512 devices in a mesh: blk: 16 (over y, core), bal: 32 (over x, z).
Axes of the slice: x: 4, y: 8, z: 8, core: 2. Of those that a mesh axis runs over, the one named last changes fastest.
Arguments:
- flow_state: float32 [64, 1024, 6, 128], P('blk', 'bal'), may hold values from -6 to 6
- source: float32 [64, 1024, 6, 128], P('blk', 'bal'), may hold values from -6 to 6
- diag_scale: float32 [64, 1024, 128], P('blk', 'bal'), may hold values from 1.5 to 6
- flux_jac: float32 [4, 6, 6], replicated, may hold values from -0.875 to 0.875
- line_coupling: float32 [2, 6, 6], replicated, may hold values from -0.625 to 0.625
- block_inverse: float32 [6, 6], replicated, may hold values from -0.15 to 1.2, as said below
- active_order: int32 [16, 32, 128], P('blk', 'bal'), may hold values from 0 to 127, each once within a row
- active_units: int32 [16, 32], P('blk', 'bal'), may hold values from 1 to 3, 64 in all within a row
- donor_cells: int32 [16, 32, 8, 16, 128], P('blk', 'bal'), may hold values from 0 to 16383
- donor_weights: float32 [16, 32, 8, 16, 128], P('blk', 'bal'), may hold values from 0.1 to 1
- receptor_cells: int32 [16, 32, 16, 128], P('blk', 'bal'), may hold values from 0 to 16383, as said below
Outputs:
- updated: float32 [64, 1024, 6, 128], P('blk', 'bal')
The draws below stay inside these ranges and needn't reach their ends.
Inputs may be any that keep to these rules, and one draw needn't show every extreme that they name: `active_order`: each grid block's list holds every local line index once. `active_units`: over the grid blocks of one row along the second dimension the units sum to exactly 64, and one of them holds 3. `donor_cells`: local cell indices within the donor's grid block. `receptor_cells`: local cell indices within the receptor's grid block, all distinct within one grid block. `block_inverse`: diagonally dominant.
All inputs are finite; a program needn't handle non-finite values.
Results may differ from the reference program's by a relative error of at most 0.0003.
Values sent between devices are 32-bit elements; how exact they have to be, the bound alone decides.
No kernel may reach another device: no remote copies, remote signals or barrier semaphores. Data moves between devices by JAX's collectives and lax.ppermute only.
A program may use at most 64 MiB of HBM per device.

```python
import math
import jax
import jax.numpy as jnp
import numpy as np
from jax import lax

FIELDS = 6
PEN = 128
CX = 4
CY = 32
SWEEPS = 4
DONORS = 8
DSLOT = 128
GX = 16
GY = 32
X = 64
Y = 1024
ROWS = 128
QUARTER = 32


def draw_block_inverse(key, part):
    key = jax.random.fold_in(key, 7)
    diag_key, off_key = jax.random.split(key)
    diagonal = jax.random.uniform(diag_key, (FIELDS,), jnp.float32, 0.8, 1.2)
    spread = jax.random.uniform(off_key, (FIELDS, FIELDS), jnp.float32, -0.15, 0.15)
    identity = jnp.eye(FIELDS, dtype=jnp.float32)
    return (identity * diagonal.reshape(1, FIELDS) + (1.0 - identity) * spread).astype(jnp.float32)


def draw_receptor_cells(key, part):
    key = jax.random.fold_in(key, 19)
    device_keys = jax.random.split(key, GX * GY)

    def choose(device_key):
        return jax.random.permutation(device_key, ROWS * PEN)[:GX * DSLOT]
    chosen = jax.vmap(choose)(device_keys)
    return chosen.reshape(GX, GY, GX, DSLOT).astype(jnp.int32)


def set_ends(result, key, low, largest):
    index_at = [jax.random.randint(jax.random.fold_in(key, axis), (), 0, length) for axis, length in enumerate(result.shape)]
    longest = result.shape.index(max(result.shape))
    beside = index_at[:longest] + [(index_at[longest] + 1) % result.shape[longest]] + index_at[longest + 1:]
    return result.at[tuple(index_at)].set(low).at[tuple(beside)].set(largest)


def block_levels(key, extent, cuts, least, largest):
    gain = 1.0
    for dim, parts in cuts:
        draws = jax.random.uniform(jax.random.fold_in(jax.random.fold_in(key, 6), dim), (parts,), jnp.float32, least / len(cuts), largest / len(cuts))
        gain = gain * jnp.repeat(jnp.exp(draws), extent[dim] // parts).reshape((-1,) + (1,) * (len(extent) - 1 - dim))
    return gain


def profile(amount, total, bound, lean):
    portions = [(1 << 20) // math.isqrt(standing ** lean) + 1 for standing in range(2, amount + 1)]
    spare, counts = total - bound - (amount - 1), [1] * (amount - 1)
    while spare > 0:
        movable = [i for i in range(amount - 1) if counts[i] < bound]
        mass, left = sum([portions[i] for i in movable]), spare
        for i in movable:
            extra = min(bound - counts[i], max(1, left * portions[i] // mass), spare)
            counts[i] = counts[i] + extra
            spare = spare - extra
    return np.array([bound] + counts)


def ragged_sizes(key, amount, total, bound, lean):
    if amount == 2:
        one = jax.random.randint(key, (), max(1, total - bound), min(bound, total - 1) + 1)
        return jnp.stack([one, total - one])
    tallies = jnp.asarray(profile(amount, total, bound, lean), jnp.int32)
    twos = (amount - 1) // 2
    giver, taker = tallies[1:1 + 2 * twos:2], tallies[2:2 + 2 * twos:2]
    room = jnp.minimum(giver - 1, bound - taker)
    moved = jax.random.randint(jax.random.fold_in(key, 1), (twos,), 0, 1 << 20) % (room + 1)
    tallies = tallies.at[1:1 + 2 * twos:2].set(giver - moved).at[2:2 + 2 * twos:2].set(taker + moved)
    return tallies[jax.random.permutation(jax.random.fold_in(key, 2), amount)]


def normal_values(rng, shape, scale, bound, pieces=(), held_as=jnp.bfloat16):
    values = jax.random.normal(rng, shape, jnp.float32) * scale
    if len(pieces) > 0:
        values = block_levels(rng, shape, pieces, -0.22, 0.18) * values
    return jnp.clip(values, min=-bound, max=bound).astype(held_as)


def setup_inputs(seed: int = 0) -> dict:
    key_of = jax.random.split(jax.random.key(seed), 12)
    return {
        "flow_state": normal_values(key_of[0], (X, Y, FIELDS, PEN), 1.0, 6.0, ((0, 16), (1, 32)), jnp.float32),
        "source": normal_values(key_of[1], (X, Y, FIELDS, PEN), 1.0, 6.0, ((0, 16), (1, 32)), jnp.float32),
        "diag_scale": jnp.clip(jnp.exp(math.log(6.0) - 1.3862944 * jax.random.uniform(key_of[2], (X, Y, PEN), jnp.float32) ** block_levels(key_of[2], (X, Y, PEN), ((0, 16), (1, 32)), -0.2, 0.2)), 1.5, 6.0),
        "flux_jac": normal_values(key_of[3], (4, FIELDS, FIELDS), 48 ** -0.5, 0.875, (), jnp.float32),
        "line_coupling": normal_values(key_of[4], (2, FIELDS, FIELDS), 96 ** -0.5, 0.625, (), jnp.float32),
        "block_inverse": draw_block_inverse(jax.random.fold_in(key_of[11], 71), 0),
        "active_order": jax.vmap(lambda own: jax.random.permutation(own, ROWS))(jax.random.split(key_of[6], GX * GY)).reshape((GX, GY, ROWS)).astype(jnp.int32),
        "active_units": jax.vmap(lambda own: ragged_sizes(own, GY, 2 * GY, 3, 0))(jax.random.split(key_of[7], GX)).reshape((GX, GY)).astype(jnp.int32),
        "donor_cells": set_ends(jax.random.randint(key_of[8], (GX, GY, DONORS, GX, DSLOT), 0, CX * CY * PEN), jax.random.fold_in(key_of[8], 1), 0, (CX * CY * PEN) - 1).astype(jnp.int32),
        "donor_weights": jnp.clip(jnp.exp(math.log(1.0) - 2.3025851 * jax.random.uniform(key_of[9], (GX, GY, DONORS, GX, DSLOT), jnp.float32) ** block_levels(key_of[9], (GX, GY, DONORS, GX, DSLOT), ((0, 16), (1, 32)), -0.2, 0.2)), 0.1, 1.0),
        "receptor_cells": draw_receptor_cells(jax.random.fold_in(key_of[11], 71), 0),
    }


def apply_block(matrix, values):
    return jnp.einsum("fg,...gp->...fp", matrix.astype(jnp.float32), values.astype(jnp.float32), precision=lax.Precision.HIGHEST)


def sweep_rows(residual, scales, coupling, inverse):
    correction = jnp.zeros_like(residual)
    for number in range(SWEEPS):
        zero_edge = jnp.zeros_like(correction[..., :1])
        below_cells = jnp.concatenate([zero_edge, correction[..., :-1]], axis=-1)
        above_cells = jnp.concatenate([correction[..., 1:], zero_edge], axis=-1)
        inner = residual - apply_block(coupling[0], below_cells) - apply_block(coupling[1], above_cells)
        correction = apply_block(inverse, inner) / scales[..., None, :]
    return correction


def interpolate(block_rows, cell_list, weights):
    fields = block_rows.shape[1]
    length = block_rows.shape[2]
    field_index = jnp.arange(fields, dtype=jnp.int32).reshape(fields, 1, 1, 1)
    picked = block_rows[(cell_list // length)[None], field_index, (cell_list % length)[None]]
    shares = weights / jnp.sum(weights, axis=0, keepdims=True)
    return jnp.sum(shares[None] * picked, axis=1)


def place(block_rows, cell_list, incoming):
    fields = block_rows.shape[1]
    length = block_rows.shape[2]
    field_index = jnp.arange(fields, dtype=jnp.int32).reshape(fields, 1, 1)
    return block_rows.at[(cell_list // length)[None], field_index, (cell_list % length)[None]].set(incoming)


def rank_of(ordering):
    return jnp.zeros((CX * CY,), jnp.int32).at[ordering].set(jnp.arange(CX * CY, dtype=jnp.int32))


def reference(flow_state, source, diag_scale, flux_jac, line_coupling, block_inverse, active_order, active_units, donor_cells, donor_weights, receptor_cells):
    ranking = jax.vmap(jax.vmap(rank_of))(active_order)
    live_rows = ranking < active_units.reshape(GX, GY, 1) * QUARTER
    live_rows = live_rows.reshape(GX, GY, CX, CY).transpose(0, 2, 1, 3).reshape(X, Y)
    padded = jnp.pad(flow_state, ((1, 1), (1, 1), (0, 0), (0, 0)))

    def one_line(line_index):
        window = lax.dynamic_slice_in_dim(padded, line_index, 3, 0)
        centre = window[1, 1:-1]
        flux_sum = apply_block(flux_jac[0], centre - window[0, 1:-1])
        flux_sum = flux_sum + apply_block(flux_jac[1], centre - window[2, 1:-1])
        flux_sum = flux_sum + apply_block(flux_jac[2], centre - window[1, :-2])
        flux_sum = flux_sum + apply_block(flux_jac[3], centre - window[1, 2:])
        residual = lax.dynamic_index_in_dim(source, line_index, 0, False) - flux_sum
        scale_line = lax.dynamic_index_in_dim(diag_scale, line_index, 0, False)
        live_line = lax.dynamic_index_in_dim(live_rows, line_index, 0, False)
        correction = sweep_rows(residual, scale_line, line_coupling, block_inverse)
        return centre + jnp.where(live_line.reshape(Y, 1, 1), correction, 0.0)

    corrected = lax.map(one_line, jnp.arange(X, dtype=jnp.int32))
    blocks = corrected.reshape(GX, CX, GY, CY, FIELDS, PEN).transpose(0, 2, 1, 3, 4, 5).reshape(GX, GY, CX * CY, FIELDS, PEN)
    values = jax.vmap(jax.vmap(interpolate))(blocks, donor_cells, donor_weights)
    arriving = values.transpose(3, 1, 2, 0, 4)
    grid_blocks = jax.vmap(jax.vmap(place))(blocks, receptor_cells, arriving)
    return grid_blocks.reshape(GX, GY, CX, CY, FIELDS, PEN).transpose(0, 2, 1, 3, 4, 5).reshape(X, Y, FIELDS, PEN)
```

```python
import functools

import jax
import jax.numpy as jnp
from jax import lax
from jax.experimental import pallas as pl
from jax.experimental.pallas import tpu as pltpu
from jax.sharding import PartitionSpec as P

SWEEPS = 4
FIELDS = 6
DONORS = 8
LANES = 128
INNER = 64
RIM = 72
NOWHERE = 255


def block_product(inverse, coupling, side):
    return [
        [
            sum(inverse[f, h] * coupling[h, side, g] for h in range(FIELDS))
            for g in range(FIELDS)
        ]
        for f in range(FIELDS)
    ]


def apply(matrix, values):
    out = []
    for f in range(FIELDS):
        total = matrix(f, 0) * values[0]
        for g in range(1, FIELDS):
            total = total + matrix(f, g) * values[g]
        out.append(total)
    return out


def solve(residual, scale_inv, inverse, below, above):
    lane = lax.broadcasted_iota(jnp.int32, residual[0].shape, 1)
    first, last = lane == 0, lane == LANES - 1
    base = apply(lambda f, g: inverse[f, g], residual)
    base = [value * scale_inv for value in base]
    correction = base
    for _ in range(SWEEPS - 1):
        total = [None] * FIELDS
        for g in range(FIELDS):
            down = jnp.where(first, 0.0, pltpu.roll(correction[g], 1, 1))
            up = jnp.where(last, 0.0, pltpu.roll(correction[g], LANES - 1, 1))
            for f in range(FIELDS):
                term = below[f][g] * down + above[f][g] * up
                total[f] = term if g == 0 else total[f] + term
        correction = [base[f] - scale_inv * total[f] for f in range(FIELDS)]
    return correction


def fill_table(table, rows, field, first, values):
    high = values.astype(jnp.bfloat16)
    low = (values - high.astype(jnp.float32)).astype(jnp.bfloat16)
    count = values.shape[0]
    table[field * rows + first : field * rows + first + count, 0:LANES] = high
    table[field * rows + first : field * rows + first + count, LANES : 2 * LANES] = low


def gather(table, rows, cells, shares, number):
    at_cell = lax.broadcasted_iota(jnp.int32, (LANES, 2 * LANES), 0)
    at_line = lax.broadcasted_iota(jnp.int32, (rows, 2 * LANES), 0)
    total = [None] * FIELDS
    for k in range(0, DONORS, 2):
        cell = jnp.concatenate([cells[k + i, pl.ds(number, 1), :] for i in (0, 1)], axis=1)
        share = jnp.concatenate([shares[k + i, pl.ds(number, 1), :] for i in (0, 1)], axis=1)
        pick = jnp.where(at_cell == (cell & (LANES - 1)), 1.0, 0.0).astype(jnp.bfloat16)
        found = jnp.dot(
            table[...], jnp.concatenate([pick, pick], axis=0), preferred_element_type=jnp.float32
        )
        weight = jnp.where(at_line == (cell >> 7), share, 0.0)
        for f in range(FIELDS):
            part = found[f * rows : (f + 1) * rows] * weight
            part = jnp.sum(part.reshape(rows // 8, 8, 2 * LANES), axis=0)
            total[f] = part if k == 0 else total[f] + part
    return [
        jnp.sum(value[:, :LANES] + value[:, LANES:], axis=0, keepdims=True) for value in total
    ]


def edges_kernel(flow, x_head, x_tail, y_head, y_tail):
    width_x, _, width_y, _ = flow.shape
    x_head[...] = flow[0]
    x_tail[...] = flow[width_x - 1]
    for f in range(FIELDS):
        for x in range(width_x):
            y_head[f, x : x + 1] = flow[x, f, 0:1]
            y_tail[f, x : x + 1] = flow[x, f, width_y - 1 : width_y]


def inner_kernel(
    jac, coupling, inverse, units, flow, source, diag, order, cells, weights,
    values, near, rim_residual, rim_scale, rim_live, rim_flow, rim_cells, shares,
    live, inner_cells, table,
):
    width_y = flow.shape[2]
    blocks = cells.shape[1]
    line = lax.broadcasted_iota(jnp.int32, (LANES, LANES), 0)
    place = lax.broadcasted_iota(jnp.int32, (LANES, LANES), 1)
    hit = (line == order[...]) & (place < units[0, 0] * 32)
    live[...] = jnp.broadcast_to(
        jnp.max(jnp.where(hit, 1.0, 0.0), axis=1, keepdims=True), (LANES, LANES)
    )
    sums = [
        [jac[f, 0, g] + jac[f, 1, g] + jac[f, 2, g] + jac[f, 3, g] for g in range(FIELDS)]
        for f in range(FIELDS)
    ]
    below = block_product(inverse, coupling, 0)
    above = block_product(inverse, coupling, 1)
    row = lax.broadcasted_iota(jnp.int32, (width_y, LANES), 0)

    cell = cells[...]
    at = cell >> 7
    x, y = at >> 5, at & 31
    middle = (x == 1) | (x == 2)
    edge = middle & ((y == 0) | (y == width_y - 1))
    pos = cell & (LANES - 1)
    inner_cells[...] = (jnp.where(middle & ~edge, at - 32, NOWHERE) << 7) + pos
    on_edge = 64 + (x - 1) + jnp.where(y == 0, 0, 2)
    on_rim = jnp.where(x == 0, at, jnp.where(x == 3, at - 64, NOWHERE))
    rim_cells[...] = (jnp.where(edge, on_edge, on_rim) << 7) + pos
    weight = weights[...]
    shares[...] = weight / jnp.sum(weight, axis=0, keepdims=True)

    def residual_of(plane):
        total = [source[plane, f] for f in range(FIELDS)]
        for g in range(FIELDS):
            here = flow[plane, g]
            left = flow[plane - 1, g] if plane > 0 else None
            right = flow[plane + 1, g] if plane < 3 else None
            before = jnp.where(row == 0, 0.0, pltpu.roll(here, 1, 0))
            after = jnp.where(row == width_y - 1, 0.0, pltpu.roll(here, width_y - 1, 0))
            for f in range(FIELDS):
                value = total[f] - sums[f][g] * here
                if left is not None:
                    value = value + jac[f, 0, g] * left
                if right is not None:
                    value = value + jac[f, 1, g] * right
                total[f] = value + jac[f, 2, g] * before + jac[f, 3, g] * after
        return total

    for number, plane in enumerate((0, 3)):
        residual = residual_of(plane)
        rows = slice(number * width_y, (number + 1) * width_y)
        for f in range(FIELDS):
            rim_residual[f, rows] = residual[f]
            rim_flow[f, rows] = flow[plane, f]
        rim_scale[rows] = 1.0 / diag[plane]
        rim_live[rows] = live[plane * width_y : (plane + 1) * width_y]
    rim_scale[RIM - 8 : RIM] = jnp.ones((8, LANES), jnp.float32)
    rim_live[RIM - 8 : RIM] = jnp.zeros((8, LANES), jnp.float32)
    for f in range(FIELDS):
        rim_residual[f, RIM - 8 : RIM] = jnp.zeros((8, LANES), jnp.float32)
        rim_flow[f, RIM - 8 : RIM] = jnp.zeros((8, LANES), jnp.float32)
    for number, plane in enumerate((1, 2)):
        residual = residual_of(plane)
        scale = 1.0 / diag[plane]
        alive = live[plane * width_y : (plane + 1) * width_y]
        for at_row, y_line in ((64 + number, 0), (66 + number, width_y - 1)):
            for f in range(FIELDS):
                rim_residual[f, at_row : at_row + 1] = residual[f][y_line : y_line + 1]
                rim_flow[f, at_row : at_row + 1] = flow[plane, f, y_line : y_line + 1]
            rim_scale[at_row : at_row + 1] = scale[y_line : y_line + 1]
            rim_live[at_row : at_row + 1] = alive[y_line : y_line + 1]
        correction = solve(residual, scale, inverse, below, above)
        for f in range(FIELDS):
            corrected = flow[plane, f] + jnp.where(alive > 0.5, correction[f], 0.0)
            near[number, f] = corrected
            fill_table(table, INNER, f, number * width_y, corrected)

    @pl.loop(0, blocks)
    def _(number):
        found = gather(table, INNER, inner_cells, shares, number)
        for f in range(FIELDS):
            values[number, f : f + 1, :] = found[f]


def rim_kernel(
    jac, coupling, inverse, x_prev, x_next, y_prev, y_next,
    part, rim_residual, rim_scale, rim_live, rim_flow, rim_cells, shares,
    values, rim, residual, table,
):
    width_y = x_prev.shape[1]
    blocks = rim_cells.shape[1]
    below = block_product(inverse, coupling, 0)
    above = block_product(inverse, coupling, 1)
    for number, (side, halo) in enumerate(((0, x_prev), (1, x_next))):
        rows = slice(number * width_y, (number + 1) * width_y)
        added = apply(lambda f, g: jac[f, side, g], [halo[g] for g in range(FIELDS)])
        for f in range(FIELDS):
            residual[f, rows] = rim_residual[f, rows] + added[f]
    for number, (side, halo) in enumerate(((2, y_prev), (3, y_next))):
        added = apply(lambda f, g: jac[f, side, g], [halo[g] for g in range(FIELDS)])
        for f in range(FIELDS):
            at_row = 64 + 2 * number
            residual[f, at_row : at_row + 2] = (
                rim_residual[f, at_row : at_row + 2] + added[f][1:3]
            )
            for at_row, x in ((number * (width_y - 1), 0), (width_y + number * (width_y - 1), 3)):
                residual[f, at_row : at_row + 1] = (
                    residual[f, at_row : at_row + 1] + added[f][x : x + 1]
                )
    for f in range(FIELDS):
        residual[f, RIM - 4 : RIM] = jnp.zeros((4, LANES), jnp.float32)
    for first in range(0, RIM, 24):
        rows = slice(first, first + 24)
        correction = solve(
            [residual[f, rows] for f in range(FIELDS)], rim_scale[rows], inverse, below, above
        )
        alive = rim_live[rows] > 0.5
        for f in range(FIELDS):
            corrected = rim_flow[f, rows] + jnp.where(alive, correction[f], 0.0)
            rim[f, rows] = corrected
            fill_table(table, RIM, f, first, corrected)

    @pl.loop(0, blocks)
    def _(number):
        found = gather(table, RIM, rim_cells, shares, number)
        for f in range(FIELDS):
            values[number, f : f + 1, :] = found[f] + part[number, f : f + 1, :]


def place_kernel(incoming, receptor, near, rim, updated, spread, pick):
    blocks = incoming.shape[0]
    width_y = near.shape[2]
    count = blocks * LANES
    at_line = lax.broadcasted_iota(jnp.int32, (INNER, LANES), 0)
    at_cell = lax.broadcasted_iota(jnp.int32, (2 * LANES, LANES), 0)
    for number in range(blocks):
        cell = receptor[number : number + 1, :]
        line = cell >> 7
        where = ((line >> 6) << 7) + (cell & (LANES - 1))
        columns = slice(number * LANES, (number + 1) * LANES)
        later = slice(count + number * LANES, count + (number + 1) * LANES)
        chosen = jnp.where(at_cell == where, 1.0, 0.0).astype(jnp.bfloat16)
        pick[:, columns] = chosen
        pick[:, later] = chosen
        mine = at_line == (line & (INNER - 1))
        for f in range(FIELDS):
            value = jnp.where(mine, incoming[number, f : f + 1, :], 0.0)
            high = value.astype(jnp.bfloat16)
            spread[f * INNER : (f + 1) * INNER, columns] = high
            spread[f * INNER : (f + 1) * INNER, later] = (
                value - high.astype(jnp.float32)
            ).astype(jnp.bfloat16)
        spread[FIELDS * INNER :, columns] = jnp.where(mine, 1.0, 0.0).astype(jnp.bfloat16)
        spread[FIELDS * INNER :, later] = jnp.zeros((INNER, LANES), jnp.bfloat16)
    placed = lax.dot_general(
        spread[...], pick[...], (((1,), (1,)), ((), ())), preferred_element_type=jnp.float32
    )
    for plane in range(4):
        rows = (plane % 2) * width_y
        lanes = slice((plane // 2) * LANES, (plane // 2 + 1) * LANES)
        taken = placed[FIELDS * INNER + rows : FIELDS * INNER + rows + width_y, lanes] > 0.5
        for f in range(FIELDS):
            value = placed[f * INNER + rows : f * INNER + rows + width_y, lanes]
            if plane in (0, 3):
                at_row = 0 if plane == 0 else width_y
                updated[plane, f] = jnp.where(taken, value, rim[f, at_row : at_row + width_y])
                continue
            updated[plane, f] = jnp.where(taken, value, near[plane - 1, f])
            for at_row, y_line in ((63 + plane, 0), (65 + plane, width_y - 1)):
                one = slice(y_line, y_line + 1)
                updated[plane, f, one] = jnp.where(
                    taken[one], value[one], rim[f, at_row : at_row + 1]
                )


def halo(ends, axis, head, tail):
    return (
        lax.ppermute(tail, axis, [(i, i + 1) for i in range(ends)]),
        lax.ppermute(head, axis, [(i + 1, i) for i in range(ends)]),
    )


def shards(
    flow_state,
    source,
    diag_scale,
    flux_jac,
    line_coupling,
    block_inverse,
    active_order,
    active_units,
    donor_cells,
    donor_weights,
    receptor_cells,
):
    f32, i32 = jnp.float32, jnp.int32
    vmem = pl.BlockSpec(memory_space=pltpu.VMEM)
    smem = pl.BlockSpec(memory_space=pltpu.SMEM)
    like = jax.ShapeDtypeStruct
    params = pltpu.CompilerParams(vmem_limit_bytes=32 << 20)
    flow = jnp.transpose(flow_state, (0, 2, 1, 3))
    source = jnp.transpose(source, (0, 2, 1, 3))
    jac = jnp.transpose(flux_jac, (1, 0, 2))
    coupling = jnp.transpose(line_coupling, (1, 0, 2))
    width_x, fields, width_y, length = flow.shape
    cells = donor_cells.reshape(donor_cells.shape[2:])
    weights = donor_weights.reshape(donor_weights.shape[2:])
    receptor = receptor_cells.reshape(receptor_cells.shape[2:])
    blocks = receptor.shape[0]

    x_head, x_tail, y_head, y_tail = pl.pallas_call(
        edges_kernel,
        out_shape=[like((fields, width_y, length), f32)] * 2
        + [like((fields, width_x, length), f32)] * 2,
        in_specs=[vmem],
        out_specs=[vmem] * 4,
        compiler_params=params,
        name="edge_lines",
    )(flow)
    x_prev, x_next = halo(lax.axis_size("blk") - 1, "blk", x_head, x_tail)
    y_prev, y_next = halo(lax.axis_size("bal") - 1, "bal", y_head, y_tail)
    part, near, *rest = pl.pallas_call(
        inner_kernel,
        out_shape=[
            like((blocks, fields, length), f32),
            like((2, fields, width_y, length), f32),
            like((fields, RIM, length), f32),
            like((RIM, length), f32),
            like((RIM, length), f32),
            like((fields, RIM, length), f32),
            like(cells.shape, i32),
            like(cells.shape, f32),
        ],
        in_specs=[smem] * 4 + [vmem] * 6,
        out_specs=[vmem] * 8,
        scratch_shapes=[
            pltpu.VMEM((LANES, LANES), f32),
            pltpu.VMEM(cells.shape, i32),
            pltpu.VMEM((fields * INNER, 2 * LANES), jnp.bfloat16),
        ],
        cost_estimate=pl.CostEstimate(
            flops=10**10, bytes_accessed=3 * 10**6, transcendentals=0
        ),
        compiler_params=params,
        name="inner_lines",
    )(
        jac, coupling, block_inverse, active_units, flow, source, diag_scale,
        active_order.reshape(1, LANES), cells, weights,
    )
    values, rim = pl.pallas_call(
        rim_kernel,
        out_shape=[
            like((blocks, fields, length), f32),
            like((fields, RIM, length), f32),
        ],
        in_specs=[smem] * 3 + [vmem] * 11,
        out_specs=[vmem] * 2,
        scratch_shapes=[
            pltpu.VMEM((fields, RIM, length), f32),
            pltpu.VMEM((fields * RIM, 2 * LANES), jnp.bfloat16),
        ],
        compiler_params=params,
        name="rim_lines",
    )(jac, coupling, block_inverse, x_prev, x_next, y_prev, y_next, part, *rest)
    incoming = lax.all_to_all(values, "blk", split_axis=0, concat_axis=0, tiled=True)
    updated = pl.pallas_call(
        place_kernel,
        out_shape=like(flow.shape, f32),
        in_specs=[vmem] * 4,
        out_specs=vmem,
        scratch_shapes=[
            pltpu.VMEM(((fields + 1) * INNER, 2 * blocks * LANES), jnp.bfloat16),
            pltpu.VMEM((2 * LANES, 2 * blocks * LANES), jnp.bfloat16),
        ],
        compiler_params=params,
        name="place_receptors",
    )(incoming, receptor, near, rim)
    return jnp.transpose(updated, (0, 2, 1, 3))


def solution(mesh):
    placed = (
        P("blk", "bal", None, None),
        P("blk", "bal", None, None),
        P("blk", "bal", None),
        P(),
        P(),
        P(),
        P("blk", "bal", None),
        P("blk", "bal"),
        P("blk", "bal", None, None, None),
        P("blk", "bal", None, None, None),
        P("blk", "bal", None, None),
    )
    return jax.shard_map(
        shards, mesh=mesh, in_specs=placed, out_specs=P("blk", "bal", None, None), check_vma=False
    )
```

```python
import functools

import jax
import jax.numpy as jnp
from jax import lax
from jax.experimental import pallas as pl
from jax.experimental.pallas import tpu as pltpu
from jax.sharding import PartitionSpec as P

SWEEPS = 4
FIELDS = 6
DONORS = 8
LANES = 128
INNER = 64
RIM = 72
NOWHERE = 255
BY_MATRIX = 4
STEPS = 1048000.0


def apply(matrix, values):
    out = []
    for f in range(FIELDS):
        total = matrix(f, 0) * values[0]
        for g in range(1, FIELDS):
            total = total + matrix(f, g) * values[g]
        out.append(total)
    return out


def solve(residual, scale_inv, matrices):
    lane = lax.broadcasted_iota(jnp.int32, residual[0].shape, 1)
    first, last = lane == 0, lane == LANES - 1
    base = apply(lambda f, g: matrices[3, f, g], residual)
    base = [value * scale_inv for value in base]
    correction = base
    for _ in range(SWEEPS - 1):
        total = [None] * FIELDS
        for g in range(FIELDS):
            down = jnp.where(first, 0.0, pltpu.roll(correction[g], 1, 1))
            up = jnp.where(last, 0.0, pltpu.roll(correction[g], LANES - 1, 1))
            for f in range(FIELDS):
                term = matrices[1, f, g] * down + matrices[2, f, g] * up
                total[f] = term if g == 0 else total[f] + term
        correction = [base[f] - scale_inv * total[f] for f in range(FIELDS)]
    return correction


def fill_table(table, rows, field, first, values):
    high = values.astype(jnp.bfloat16)
    low = (values - high.astype(jnp.float32)).astype(jnp.bfloat16)
    count = values.shape[0]
    table[field * rows + first : field * rows + first + count, 0:LANES] = high
    table[field * rows + first : field * rows + first + count, LANES : 2 * LANES] = low


def fill_words(words, scales, corrected):
    whole = []
    for f in range(FIELDS):
        largest = jnp.max(jnp.max(jnp.abs(corrected(f)), axis=0, keepdims=True), axis=1, keepdims=True)
        scale = jnp.broadcast_to(jnp.maximum(largest, 1e-30), (8, LANES))
        scales[f] = scale * (1.0 / (STEPS * 2048.0))
        factor = (STEPS / scale)[0:1]
        whole.append(jnp.round(corrected(f) * factor).astype(jnp.int32))
    parts = []
    for f in (4, 5):
        upper = (whole[f] + 512) >> 10
        parts += [upper, whole[f] - (upper << 10)]
    for word in range(4):
        words[word] = (whole[word] << 11) + parts[word]


def gather_by_lane(words, rows, cell, share, total):
    below = lax.broadcasted_iota(jnp.int32, (8, LANES), 0)
    cell = jnp.broadcast_to(cell, (8, LANES))
    pos = cell & (LANES - 1)
    line = (cell >> 7) - below
    here = ((line & 7) == 0) & (line < rows) & (line >= 0)
    share = jnp.where(here, jnp.broadcast_to(share, (8, LANES)), 0.0)
    hit = [None] * 4
    for first in range(0, rows, 8):
        chosen = line == first
        for word in range(4):
            found = jnp.take_along_axis(
                words[word, first : first + 8], pos, axis=1, mode="promise_in_bounds"
            )
            hit[word] = found if first == 0 else jnp.where(chosen, found, hit[word])
    low = [(value << 21).astype(jnp.float32) for value in hit]
    found = [value.astype(jnp.float32) for value in hit]
    found += [low[0] + low[1] * (1.0 / 1024), low[2] + low[3] * (1.0 / 1024)]
    return [
        value * share if total is None else total[f] + value * share
        for f, value in enumerate(found)
    ]


def small(numbers):
    return numbers.astype(jnp.float32).astype(jnp.bfloat16)


def gather(table, words, scales, rows, cells, shares, number):
    at_cell = small(lax.broadcasted_iota(jnp.int32, (LANES, 2 * LANES), 0))
    at_line = lax.broadcasted_iota(jnp.int32, (rows, 2 * LANES), 0)
    one, zero = jnp.bfloat16(1), jnp.bfloat16(0)
    total = [None] * FIELDS
    for k in range(0, BY_MATRIX, 2):
        cell = jnp.concatenate([cells[k + i, pl.ds(number, 1), :] for i in (0, 1)], axis=1)
        share = jnp.concatenate([shares[k + i, pl.ds(number, 1), :] for i in (0, 1)], axis=1)
        pick = jnp.where(at_cell == small(cell & (LANES - 1)), one, zero)
        found = jnp.dot(
            table[...], jnp.concatenate([pick, pick], axis=0), preferred_element_type=jnp.float32
        )
        weight = jnp.where(at_line == (cell >> 7), share, 0.0)
        for f in range(FIELDS):
            part = found[f * rows : (f + 1) * rows] * weight
            part = jnp.sum(part.reshape(rows // 8, 8, 2 * LANES), axis=0)
            total[f] = part if k == 0 else total[f] + part
    by_lane = None
    for k in range(BY_MATRIX, DONORS):
        by_lane = gather_by_lane(
            words, rows, cells[k, pl.ds(number, 1), :], shares[k, pl.ds(number, 1), :], by_lane
        )
    return [
        jnp.sum(
            value[:, :LANES] + value[:, LANES:] + by_lane[f] * scales[f], axis=0, keepdims=True
        )
        for f, value in enumerate(total)
    ]


def load_kernel(
    jac_in, coupling_in, inverse_in, flow_in, source_in, diag_in, cells_in, weights_in,
    x_head, x_tail, y_head, y_tail, flow, source, diag, cells, weights, matrices,
    jac, coupling, inverse, done,
):
    width_x, _, width_y, _ = flow.shape
    copies = [
        pltpu.make_async_copy(origin, target, done.at[number])
        for number, (origin, target) in enumerate(
            (
                (flow_in, flow),
                (jac_in, jac),
                (coupling_in, coupling),
                (inverse_in, inverse),
                (flow_in.at[0], x_head),
                (flow_in.at[width_x - 1], x_tail),
                (source_in, source),
                (diag_in, diag),
                (cells_in, cells),
                (weights_in, weights),
            )
        )
    ]
    for copy in copies:
        copy.start()
    for copy in copies[1:4]:
        copy.wait()
    for f in range(FIELDS):
        for g in range(FIELDS):
            for side in range(4):
                matrices[4 + side, f, g] = jac[f, side, g]
            matrices[0, f, g] = jac[f, 0, g] + jac[f, 1, g] + jac[f, 2, g] + jac[f, 3, g]
            matrices[3, f, g] = inverse[f, g]
            for side in (0, 1):
                total = inverse[f, 0] * coupling[0, side, g]
                for h in range(1, FIELDS):
                    total = total + inverse[f, h] * coupling[h, side, g]
                matrices[1 + side, f, g] = total
    copies[0].wait()
    for f in range(FIELDS):
        for x in range(width_x):
            y_head[f, x : x + 1] = flow[x, f, 0:1]
            y_tail[f, x : x + 1] = flow[x, f, width_y - 1 : width_y]
    for copy in copies[4:]:
        copy.wait()


def inner_kernel(
    matrices, units, flow, source, diag, order, cells, weights,
    values, near, rim_residual, rim_scale, rim_live, rim_flow, rim_cells, shares,
    live, inner_cells, table, words, scales,
):
    width_y = flow.shape[2]
    blocks = cells.shape[1]
    line = lax.broadcasted_iota(jnp.int32, (LANES, LANES), 0)
    place = lax.broadcasted_iota(jnp.int32, (LANES, LANES), 1)
    hit = (line == order[...]) & (place < units[0, 0] * 32)
    live[...] = jnp.broadcast_to(
        jnp.max(jnp.where(hit, 1.0, 0.0), axis=1, keepdims=True), (LANES, LANES)
    )
    row = lax.broadcasted_iota(jnp.int32, (width_y, LANES), 0)

    cell = cells[...]
    at = cell >> 7
    x, y = at >> 5, at & 31
    middle = (x == 1) | (x == 2)
    edge = middle & ((y == 0) | (y == width_y - 1))
    pos = cell & (LANES - 1)
    inner_cells[...] = (jnp.where(middle & ~edge, at - 32, NOWHERE) << 7) + pos
    on_edge = 64 + (x - 1) + jnp.where(y == 0, 0, 2)
    on_rim = jnp.where(x == 0, at, jnp.where(x == 3, at - 64, NOWHERE))
    rim_cells[...] = (jnp.where(edge, on_edge, on_rim) << 7) + pos
    weight = weights[...]
    shares[...] = weight / jnp.sum(weight, axis=0, keepdims=True)

    def residual_of(plane):
        total = [source[plane, f] for f in range(FIELDS)]
        for g in range(FIELDS):
            here = flow[plane, g]
            left = flow[plane - 1, g] if plane > 0 else None
            right = flow[plane + 1, g] if plane < 3 else None
            before = jnp.where(row == 0, 0.0, pltpu.roll(here, 1, 0))
            after = jnp.where(row == width_y - 1, 0.0, pltpu.roll(here, width_y - 1, 0))
            for f in range(FIELDS):
                value = total[f] - matrices[0, f, g] * here
                if left is not None:
                    value = value + matrices[4, f, g] * left
                if right is not None:
                    value = value + matrices[5, f, g] * right
                total[f] = value + matrices[6, f, g] * before + matrices[7, f, g] * after
        return total

    for number, plane in enumerate((0, 3)):
        residual = residual_of(plane)
        rows = slice(number * width_y, (number + 1) * width_y)
        for f in range(FIELDS):
            rim_residual[f, rows] = residual[f]
            rim_flow[f, rows] = flow[plane, f]
        rim_scale[rows] = 1.0 / diag[plane]
        rim_live[rows] = live[plane * width_y : (plane + 1) * width_y]
    rim_scale[RIM - 8 : RIM] = jnp.ones((8, LANES), jnp.float32)
    rim_live[RIM - 8 : RIM] = jnp.zeros((8, LANES), jnp.float32)
    for f in range(FIELDS):
        rim_residual[f, RIM - 8 : RIM] = jnp.zeros((8, LANES), jnp.float32)
        rim_flow[f, RIM - 8 : RIM] = jnp.zeros((8, LANES), jnp.float32)
    for number, plane in enumerate((1, 2)):
        residual = residual_of(plane)
        scale = 1.0 / diag[plane]
        alive = live[plane * width_y : (plane + 1) * width_y]
        for at_row, y_line in ((64 + number, 0), (66 + number, width_y - 1)):
            for f in range(FIELDS):
                rim_residual[f, at_row : at_row + 1] = residual[f][y_line : y_line + 1]
                rim_flow[f, at_row : at_row + 1] = flow[plane, f, y_line : y_line + 1]
            rim_scale[at_row : at_row + 1] = scale[y_line : y_line + 1]
            rim_live[at_row : at_row + 1] = alive[y_line : y_line + 1]
        correction = solve(residual, scale, matrices)
        for f in range(FIELDS):
            corrected = flow[plane, f] + jnp.where(alive > 0.5, correction[f], 0.0)
            near[number, f] = corrected
            fill_table(table, INNER, f, number * width_y, corrected)

    fill_words(
        words, scales, lambda f: jnp.concatenate([near[0, f], near[1, f]], axis=0)
    )

    @pl.loop(0, blocks, unroll=4)
    def _(number):
        found = gather(table, words, scales, INNER, inner_cells, shares, number)
        for f in range(FIELDS):
            values[number, f : f + 1, :] = found[f]


def rim_kernel(
    matrices, x_prev, x_next, y_prev, y_next,
    part, rim_residual, rim_scale, rim_live, rim_flow, rim_cells, shares,
    values, rim, residual, table, words, scales,
):
    width_y = x_prev.shape[1]
    blocks = rim_cells.shape[1]
    for number, (side, halo) in enumerate(((0, x_prev), (1, x_next))):
        rows = slice(number * width_y, (number + 1) * width_y)
        added = apply(lambda f, g: matrices[4 + side, f, g], [halo[g] for g in range(FIELDS)])
        for f in range(FIELDS):
            residual[f, rows] = rim_residual[f, rows] + added[f]
    for number, (side, halo) in enumerate(((2, y_prev), (3, y_next))):
        added = apply(lambda f, g: matrices[4 + side, f, g], [halo[g] for g in range(FIELDS)])
        for f in range(FIELDS):
            at_row = 64 + 2 * number
            residual[f, at_row : at_row + 2] = (
                rim_residual[f, at_row : at_row + 2] + added[f][1:3]
            )
            for at_row, x in ((number * (width_y - 1), 0), (width_y + number * (width_y - 1), 3)):
                residual[f, at_row : at_row + 1] = (
                    residual[f, at_row : at_row + 1] + added[f][x : x + 1]
                )
    for f in range(FIELDS):
        residual[f, RIM - 4 : RIM] = jnp.zeros((4, LANES), jnp.float32)
    for first in range(0, RIM, 24):
        rows = slice(first, first + 24)
        correction = solve(
            [residual[f, rows] for f in range(FIELDS)], rim_scale[rows], matrices
        )
        alive = rim_live[rows] > 0.5
        for f in range(FIELDS):
            corrected = rim_flow[f, rows] + jnp.where(alive, correction[f], 0.0)
            rim[f, rows] = corrected
            fill_table(table, RIM, f, first, corrected)

    fill_words(words, scales, lambda f: rim[f])

    @pl.loop(0, blocks, unroll=4)
    def _(number):
        found = gather(table, words, scales, RIM, rim_cells, shares, number)
        for f in range(FIELDS):
            values[number, f : f + 1, :] = found[f] + part[number, f : f + 1, :]


def prepare_kernel(receptor, near, rim, base, lines, pick):
    blocks = receptor.shape[0]
    width_y = near.shape[2]
    at_line = lax.broadcasted_iota(jnp.int32, (INNER, LANES), 0)
    at_cell = lax.broadcasted_iota(jnp.int32, (LANES, LANES), 1)
    for number in range(blocks):
        cell = receptor[number : number + 1, :]
        line = cell >> 7
        where = ((line >> 6) << 7) + (cell & (LANES - 1))
        span = slice(number * LANES, (number + 1) * LANES)
        lines[:, span] = jnp.where(at_line == (line & (INNER - 1)), 1.0, 0.0).astype(jnp.bfloat16)
        where = jnp.transpose(jnp.broadcast_to(where, (LANES, LANES)))
        for half in (0, 1):
            pick[span, half * LANES : (half + 1) * LANES] = jnp.where(
                at_cell + half * LANES == where, 1.0, 0.0
            ).astype(jnp.bfloat16)
    taken = jnp.dot(lines[...], pick[...], preferred_element_type=jnp.float32)
    for plane in range(4):
        rows = (plane % 2) * width_y
        lanes = slice((plane // 2) * LANES, (plane // 2 + 1) * LANES)
        free = taken[rows : rows + width_y, lanes] < 0.5
        for f in range(FIELDS):
            if plane in (0, 3):
                at_row = 0 if plane == 0 else width_y
                base[plane, f] = jnp.where(free, rim[f, at_row : at_row + width_y], 0.0)
                continue
            base[plane, f] = jnp.where(free, near[plane - 1, f], 0.0)
            for at_row, y_line in ((63 + plane, 0), (65 + plane, width_y - 1)):
                one = slice(y_line, y_line + 1)
                base[plane, f, one] = jnp.where(free[one], rim[f, at_row : at_row + 1], 0.0)


def place_kernel(incoming, base, lines, pick, updated, high, low):
    blocks = incoming.shape[0]
    width_y = base.shape[2]
    for number in range(blocks):
        span = slice(number * LANES, (number + 1) * LANES)
        value = incoming[number]
        upper = value.astype(jnp.bfloat16).astype(jnp.float32)
        lower = value - upper
        for f in range(FIELDS):
            for part, target in ((upper, high), (lower, low)):
                wide = jnp.broadcast_to(part[f : f + 1], (16, LANES)).astype(jnp.bfloat16)
                for first in range(0, INNER, 16):
                    target[f * INNER + first : f * INNER + first + 16, span] = (
                        lines[first : first + 16, span] * wide
                    )
    placed = jnp.dot(high[...], pick[...], preferred_element_type=jnp.float32)
    placed = placed + jnp.dot(low[...], pick[...], preferred_element_type=jnp.float32)
    for plane in range(4):
        rows = (plane % 2) * width_y
        lanes = slice((plane // 2) * LANES, (plane // 2 + 1) * LANES)
        for f in range(FIELDS):
            updated[plane, f] = (
                base[plane, f] + placed[f * INNER + rows : f * INNER + rows + width_y, lanes]
            )


def halo(ends, axis, head, tail):
    return (
        lax.ppermute(tail, axis, [(i, i + 1) for i in range(ends)]),
        lax.ppermute(head, axis, [(i + 1, i) for i in range(ends)]),
    )


def shards(
    flow_state,
    source,
    diag_scale,
    flux_jac,
    line_coupling,
    block_inverse,
    active_order,
    active_units,
    donor_cells,
    donor_weights,
    receptor_cells,
):
    f32, i32 = jnp.float32, jnp.int32
    vmem = pl.BlockSpec(memory_space=pltpu.VMEM)
    smem = pl.BlockSpec(memory_space=pltpu.SMEM)
    like = jax.ShapeDtypeStruct
    params = pltpu.CompilerParams(vmem_limit_bytes=32 << 20)
    flow = jnp.transpose(flow_state, (0, 2, 1, 3))
    source = jnp.transpose(source, (0, 2, 1, 3))
    jac = jnp.transpose(flux_jac, (1, 0, 2))
    coupling = jnp.transpose(line_coupling, (1, 0, 2))
    width_x, fields, width_y, length = flow.shape
    cells = donor_cells.reshape(donor_cells.shape[2:])
    weights = donor_weights.reshape(donor_weights.shape[2:])
    receptor = receptor_cells.reshape(receptor_cells.shape[2:])
    blocks = receptor.shape[0]

    outside = pl.BlockSpec(memory_space=pltpu.HBM)
    raw = [
        pltpu.with_memory_space_constraint(array, pltpu.HBM)
        for array in (jac, coupling, block_inverse, flow, source, diag_scale, cells, weights)
    ]
    x_head, x_tail, y_head, y_tail, flow, source, diag, cells, weights, matrices = pl.pallas_call(
        load_kernel,
        out_shape=[like((fields, width_y, length), f32)] * 2
        + [like((fields, width_x, length), f32)] * 2
        + [like(array.shape, array.dtype) for array in raw[3:]]
        + [like((8, fields, fields), f32)],
        in_specs=[outside] * 8,
        out_specs=[vmem] * 9 + [smem],
        scratch_shapes=[
            pltpu.SMEM(jac.shape, f32),
            pltpu.SMEM(coupling.shape, f32),
            pltpu.SMEM(block_inverse.shape, f32),
            pltpu.SemaphoreType.DMA((10,)),
        ],
        compiler_params=params,
        name="load_block",
    )(*raw)
    x_prev, x_next = halo(lax.axis_size("blk") - 1, "blk", x_head, x_tail)
    y_prev, y_next = halo(lax.axis_size("bal") - 1, "bal", y_head, y_tail)
    part, near, *rest = pl.pallas_call(
        inner_kernel,
        out_shape=[
            like((blocks, fields, length), f32),
            like((2, fields, width_y, length), f32),
            like((fields, RIM, length), f32),
            like((RIM, length), f32),
            like((RIM, length), f32),
            like((fields, RIM, length), f32),
            like(cells.shape, i32),
            like(cells.shape, f32),
        ],
        in_specs=[smem] * 2 + [vmem] * 6,
        out_specs=[vmem] * 8,
        scratch_shapes=[
            pltpu.VMEM((LANES, LANES), f32),
            pltpu.VMEM(cells.shape, i32),
            pltpu.VMEM((fields * INNER, 2 * LANES), jnp.bfloat16),
            pltpu.VMEM((4, INNER, LANES), i32),
            pltpu.VMEM((fields, 8, LANES), f32),
        ],
        cost_estimate=pl.CostEstimate(
            flops=10**10, bytes_accessed=3 * 10**6, transcendentals=0
        ),
        compiler_params=params,
        name="inner_lines",
    )(
        matrices, active_units, flow, source, diag,
        active_order.reshape(1, LANES), cells, weights,
    )
    values, rim = pl.pallas_call(
        rim_kernel,
        out_shape=[
            like((blocks, fields, length), f32),
            like((fields, RIM, length), f32),
        ],
        in_specs=[smem] + [vmem] * 11,
        out_specs=[vmem] * 2,
        scratch_shapes=[
            pltpu.VMEM((fields, RIM, length), f32),
            pltpu.VMEM((fields * RIM, 2 * LANES), jnp.bfloat16),
            pltpu.VMEM((4, RIM, LANES), i32),
            pltpu.VMEM((fields, 8, LANES), f32),
        ],
        compiler_params=params,
        name="rim_lines",
    )(matrices, x_prev, x_next, y_prev, y_next, part, *rest)
    incoming = lax.all_to_all(values, "blk", split_axis=0, concat_axis=0, tiled=True)
    base, lines, pick = pl.pallas_call(
        prepare_kernel,
        out_shape=[
            like(flow.shape, f32),
            like((INNER, blocks * LANES), jnp.bfloat16),
            like((blocks * LANES, 2 * LANES), jnp.bfloat16),
        ],
        in_specs=[vmem] * 3,
        out_specs=[vmem] * 3,
        cost_estimate=pl.CostEstimate(
            flops=5 * 10**9, bytes_accessed=3 * 10**6, transcendentals=0
        ),
        compiler_params=params,
        name="prepare_receptors",
    )(receptor, near, rim)
    updated = pl.pallas_call(
        place_kernel,
        out_shape=like(flow.shape, f32),
        in_specs=[vmem] * 4,
        out_specs=vmem,
        scratch_shapes=[pltpu.VMEM((fields * INNER, blocks * LANES), jnp.bfloat16)] * 2,
        compiler_params=params,
        name="place_receptors",
    )(incoming, base, lines, pick)
    return jnp.transpose(updated, (0, 2, 1, 3))


def solution(mesh):
    placed = (
        P("blk", "bal", None, None),
        P("blk", "bal", None, None),
        P("blk", "bal", None),
        P(),
        P(),
        P(),
        P("blk", "bal", None),
        P("blk", "bal"),
        P("blk", "bal", None, None, None),
        P("blk", "bal", None, None, None),
        P("blk", "bal", None, None),
    )
    return jax.shard_map(
        shards, mesh=mesh, in_specs=placed, out_specs=P("blk", "bal", None, None), check_vma=False
    )
```

```python
import functools

import jax
import jax.numpy as jnp
from jax import lax
from jax.experimental import pallas as pl
from jax.experimental.pallas import tpu as pltpu
from jax.sharding import PartitionSpec as P

SWEEPS = 4
FIELDS = 6
DONORS = 8
LANES = 128
INNER = 64
RIM = 72
HALF = 32
BY_MATRIX = 4
STEPS = 1048000.0


def apply(matrix, values):
    out = []
    for f in range(FIELDS):
        total = matrix(f, 0) * values[0]
        for g in range(1, FIELDS):
            total = total + matrix(f, g) * values[g]
        out.append(total)
    return out


def solve(residual, scale_inv, matrices):
    lane = lax.broadcasted_iota(jnp.int32, residual[0].shape, 1)
    first, last = lane == 0, lane == LANES - 1
    base = apply(lambda f, g: matrices[3, f, g], residual)
    base = [value * scale_inv for value in base]
    correction = base
    for _ in range(SWEEPS - 1):
        total = [None] * FIELDS
        for g in range(FIELDS):
            down = jnp.where(first, 0.0, pltpu.roll(correction[g], 1, 1))
            up = jnp.where(last, 0.0, pltpu.roll(correction[g], LANES - 1, 1))
            for f in range(FIELDS):
                term = matrices[1, f, g] * down + matrices[2, f, g] * up
                total[f] = term if g == 0 else total[f] + term
        correction = [base[f] - scale_inv * total[f] for f in range(FIELDS)]
    return correction


def fill_table(table, first, half, values):
    high = values.astype(jnp.bfloat16)
    low = (values - high.astype(jnp.float32)).astype(jnp.bfloat16)
    rows = slice(first, first + values.shape[0])
    table[rows, half * LANES : (half + 1) * LANES] = high
    table[rows, (half + 2) * LANES : (half + 3) * LANES] = low


def fill_words(words, scales, corrected):
    whole = []
    for f in range(FIELDS):
        largest = jnp.max(jnp.max(jnp.abs(corrected(f)), axis=0, keepdims=True), axis=1, keepdims=True)
        scale = jnp.broadcast_to(jnp.maximum(largest, 1e-30), (8, LANES))
        scales[f] = scale * (1.0 / (STEPS * 2048.0))
        factor = (STEPS / scale)[0:1]
        whole.append(jnp.round(corrected(f) * factor).astype(jnp.int32))
    parts = []
    for f in (4, 5):
        upper = (whole[f] + 512) >> 10
        parts += [upper, whole[f] - (upper << 10)]
    for word in range(4):
        words[word] = (whole[word] << 11) + parts[word]


def gather_by_lane(words, rows, cell, share, total):
    below = lax.broadcasted_iota(jnp.int32, (8, LANES), 0)
    cell = jnp.broadcast_to(cell, (8, LANES))
    pos = cell & (LANES - 1)
    line = (cell >> 7) - below
    share = jnp.where((line & 7) == 0, jnp.broadcast_to(share, (8, LANES)), 0.0)
    hit = [None] * 4
    for first in range(0, rows, 8):
        chosen = line == first
        for word in range(4):
            found = jnp.take_along_axis(
                words[word, first : first + 8], pos, axis=1, mode="promise_in_bounds"
            )
            hit[word] = found if first == 0 else jnp.where(chosen, found, hit[word])
    low = [(value << 21).astype(jnp.float32) for value in hit]
    found = [value.astype(jnp.float32) for value in hit]
    found += [low[0] + low[1] * (1.0 / 1024), low[2] + low[3] * (1.0 / 1024)]
    return [
        value * share if total is None else total[f] + value * share
        for f, value in enumerate(found)
    ]


def small(numbers):
    return numbers.astype(jnp.float32).astype(jnp.bfloat16)


def gather(table, words, scales, rows, cells, shares, number):
    at_cell = small(lax.broadcasted_iota(jnp.int32, (2 * LANES, 2 * LANES), 0))
    at_line = lax.broadcasted_iota(jnp.int32, (rows - HALF, 2 * LANES), 0)
    one, zero = jnp.bfloat16(1), jnp.bfloat16(0)
    extra = rows - 2 * HALF
    total = [None] * FIELDS
    for k in range(0, BY_MATRIX, 2):
        cell = jnp.concatenate([cells[k + i, pl.ds(number, 1), :] for i in (0, 1)], axis=1)
        share = jnp.concatenate([shares[k + i, pl.ds(number, 1), :] for i in (0, 1)], axis=1)
        column = ((cell >> 5) & LANES) + (cell & (LANES - 1))
        line = ((cell >> 7) & (HALF - 1)) + ((cell >> 8) & HALF)
        pick = jnp.where(at_cell == small(column), one, zero)
        found = jnp.dot(
            table[...], jnp.concatenate([pick, pick], axis=0), preferred_element_type=jnp.float32
        )
        weight = jnp.where(at_line == line, share, 0.0)
        for f in range(FIELDS):
            part = found[f * HALF : (f + 1) * HALF] * weight[:HALF]
            part = jnp.sum(part.reshape(HALF // 8, 8, 2 * LANES), axis=0)
            if extra:
                first = FIELDS * HALF + f * extra
                part = part + found[first : first + extra] * weight[HALF:]
            total[f] = part if k == 0 else total[f] + part
    by_lane = None
    for k in range(BY_MATRIX, DONORS):
        by_lane = gather_by_lane(
            words, rows, cells[k, pl.ds(number, 1), :], shares[k, pl.ds(number, 1), :], by_lane
        )
    return [
        jnp.sum(
            value[:, :LANES] + value[:, LANES:] + by_lane[f] * scales[f], axis=0, keepdims=True
        )
        for f, value in enumerate(total)
    ]


def prepare(receptor, lines, pick, taken):
    at_line = lax.broadcasted_iota(jnp.int32, (INNER, LANES), 0)
    at_cell = lax.broadcasted_iota(jnp.int32, (LANES, LANES), 1)
    for number in range(receptor.shape[0]):
        cell = receptor[number : number + 1, :]
        line = cell >> 7
        where = ((line >> 6) << 7) + (cell & (LANES - 1))
        span = slice(number * LANES, (number + 1) * LANES)
        lines[:, span] = jnp.where(at_line == (line & (INNER - 1)), 1.0, 0.0).astype(jnp.bfloat16)
        where = jnp.transpose(jnp.broadcast_to(where, (LANES, LANES)))
        for half in (0, 1):
            pick[span, half * LANES : (half + 1) * LANES] = jnp.where(
                at_cell + half * LANES == where, 1.0, 0.0
            ).astype(jnp.bfloat16)
    taken[...] = jnp.dot(lines[...], pick[...], preferred_element_type=jnp.float32)


def load_kernel(
    jac_in, coupling_in, inverse_in, units_in, order_in, receptor_in,
    flow_in, source_in, diag_in, cells_in, weights_in,
    x_head, x_tail, y_head, y_tail, flow, source, diag, cells, weights,
    live, lines, pick, taken, matrices,
    jac, coupling, inverse, units, order, receptor, done,
):
    width_x, _, width_y, _ = flow.shape
    copies = [
        pltpu.make_async_copy(origin, target, done.at[number])
        for number, (origin, target) in enumerate(
            (
                (jac_in, jac),
                (coupling_in, coupling),
                (inverse_in, inverse),
                (units_in, units),
                (order_in, order),
                (receptor_in, receptor),
                (flow_in, flow),
                (flow_in.at[0], x_head),
                (flow_in.at[width_x - 1], x_tail),
                (source_in, source),
                (diag_in, diag),
                (cells_in, cells),
                (weights_in, weights),
            )
        )
    ]
    for copy in copies:
        copy.start()
    for copy in copies[:6]:
        copy.wait()
    for f in range(FIELDS):
        for g in range(FIELDS):
            for side in range(4):
                matrices[4 + side, f, g] = jac[f, side, g]
            matrices[0, f, g] = jac[f, 0, g] + jac[f, 1, g] + jac[f, 2, g] + jac[f, 3, g]
            matrices[3, f, g] = inverse[f, g]
            for side in (0, 1):
                total = inverse[f, 0] * coupling[0, side, g]
                for h in range(1, FIELDS):
                    total = total + inverse[f, h] * coupling[h, side, g]
                matrices[1 + side, f, g] = total
    line = lax.broadcasted_iota(jnp.int32, (LANES, LANES), 0)
    place = lax.broadcasted_iota(jnp.int32, (LANES, LANES), 1)
    hit = (line == order[...]) & (place < units[0, 0] * 32)
    live[...] = jnp.broadcast_to(
        jnp.max(jnp.where(hit, 1.0, 0.0), axis=1, keepdims=True), (LANES, LANES)
    )
    prepare(receptor, lines, pick, taken)
    copies[6].wait()
    for f in range(FIELDS):
        for x in range(width_x):
            y_head[f, x : x + 1] = flow[x, f, 0:1]
            y_tail[f, x : x + 1] = flow[x, f, width_y - 1 : width_y]
    for copy in copies[7:]:
        copy.wait()


def inner_kernel(
    matrices, flow, source, diag, live, cells, weights,
    values, near, rim_residual, rim_scale, rim_live, rim_flow, rim_cells, rim_shares,
    inner_cells, inner_shares, table, words, scales,
):
    width_y = flow.shape[2]
    blocks = cells.shape[1]
    row = lax.broadcasted_iota(jnp.int32, (width_y, LANES), 0)

    cell = cells[...]
    at = cell >> 7
    x, y = at >> 5, at & 31
    middle = (x == 1) | (x == 2)
    edge = middle & ((y == 0) | (y == width_y - 1))
    pos = cell & (LANES - 1)
    inner = middle & ~edge
    inner_cells[...] = (((at - 32) & (INNER - 1)) << 7) + pos
    on_edge = 64 + (x - 1) + jnp.where(y == 0, 0, 2)
    on_rim = jnp.where(x == 0, at, (at - 64) & 63)
    rim_cells[...] = (jnp.where(edge, on_edge, on_rim) << 7) + pos
    weight = weights[...]
    share = weight / jnp.sum(weight, axis=0, keepdims=True)
    inner_shares[...] = jnp.where(inner, share, 0.0)
    rim_shares[...] = jnp.where(inner, 0.0, share)

    def residual_of(plane):
        total = [source[plane, f] for f in range(FIELDS)]
        for g in range(FIELDS):
            here = flow[plane, g]
            left = flow[plane - 1, g] if plane > 0 else None
            right = flow[plane + 1, g] if plane < 3 else None
            before = jnp.where(row == 0, 0.0, pltpu.roll(here, 1, 0))
            after = jnp.where(row == width_y - 1, 0.0, pltpu.roll(here, width_y - 1, 0))
            for f in range(FIELDS):
                value = total[f] - matrices[0, f, g] * here
                if left is not None:
                    value = value + matrices[4, f, g] * left
                if right is not None:
                    value = value + matrices[5, f, g] * right
                total[f] = value + matrices[6, f, g] * before + matrices[7, f, g] * after
        return total

    for number, plane in enumerate((0, 3)):
        residual = residual_of(plane)
        rows = slice(number * width_y, (number + 1) * width_y)
        for f in range(FIELDS):
            rim_residual[f, rows] = residual[f]
            rim_flow[f, rows] = flow[plane, f]
        rim_scale[rows] = 1.0 / diag[plane]
        rim_live[rows] = live[plane * width_y : (plane + 1) * width_y]
    rim_scale[RIM - 8 : RIM] = jnp.ones((8, LANES), jnp.float32)
    rim_live[RIM - 8 : RIM] = jnp.zeros((8, LANES), jnp.float32)
    for f in range(FIELDS):
        rim_residual[f, RIM - 8 : RIM] = jnp.zeros((8, LANES), jnp.float32)
        rim_flow[f, RIM - 8 : RIM] = jnp.zeros((8, LANES), jnp.float32)
    for number, plane in enumerate((1, 2)):
        residual = residual_of(plane)
        scale = 1.0 / diag[plane]
        alive = live[plane * width_y : (plane + 1) * width_y]
        for at_row, y_line in ((64 + number, 0), (66 + number, width_y - 1)):
            for f in range(FIELDS):
                rim_residual[f, at_row : at_row + 1] = residual[f][y_line : y_line + 1]
                rim_flow[f, at_row : at_row + 1] = flow[plane, f, y_line : y_line + 1]
            rim_scale[at_row : at_row + 1] = scale[y_line : y_line + 1]
            rim_live[at_row : at_row + 1] = alive[y_line : y_line + 1]
        correction = solve(residual, scale, matrices)
        for f in range(FIELDS):
            corrected = flow[plane, f] + jnp.where(alive > 0.5, correction[f], 0.0)
            near[number, f] = corrected
            fill_table(table, f * HALF, number, corrected)

    fill_words(
        words, scales, lambda f: jnp.concatenate([near[0, f], near[1, f]], axis=0)
    )

    @pl.loop(0, blocks, unroll=8)
    def _(number):
        found = gather(table, words, scales, INNER, inner_cells, inner_shares, number)
        for f in range(FIELDS):
            values[number, f : f + 1, :] = found[f]


def rim_kernel(
    matrices, x_prev, x_next, y_prev, y_next,
    part, rim_residual, rim_scale, rim_live, rim_flow, rim_cells, shares,
    values, rim, residual, table, words, scales,
):
    width_y = x_prev.shape[1]
    blocks = rim_cells.shape[1]
    for number, (side, halo) in enumerate(((0, x_prev), (1, x_next))):
        rows = slice(number * width_y, (number + 1) * width_y)
        added = apply(lambda f, g: matrices[4 + side, f, g], [halo[g] for g in range(FIELDS)])
        for f in range(FIELDS):
            residual[f, rows] = rim_residual[f, rows] + added[f]
    for number, (side, halo) in enumerate(((2, y_prev), (3, y_next))):
        added = apply(lambda f, g: matrices[4 + side, f, g], [halo[g] for g in range(FIELDS)])
        for f in range(FIELDS):
            at_row = 64 + 2 * number
            residual[f, at_row : at_row + 2] = (
                rim_residual[f, at_row : at_row + 2] + added[f][1:3]
            )
            for at_row, x in ((number * (width_y - 1), 0), (width_y + number * (width_y - 1), 3)):
                residual[f, at_row : at_row + 1] = (
                    residual[f, at_row : at_row + 1] + added[f][x : x + 1]
                )
    for f in range(FIELDS):
        residual[f, RIM - 4 : RIM] = jnp.zeros((4, LANES), jnp.float32)
    edges = []
    for half, rows in enumerate((slice(0, 32), slice(32, 64), slice(64, RIM))):
        correction = solve(
            [residual[f, rows] for f in range(FIELDS)], rim_scale[rows], matrices
        )
        alive = rim_live[rows] > 0.5
        for f in range(FIELDS):
            corrected = rim_flow[f, rows] + jnp.where(alive, correction[f], 0.0)
            rim[f, rows] = corrected
            if half < 2:
                fill_table(table, f * HALF, half, corrected)
            else:
                edges.append(corrected)
    edges = jnp.concatenate(edges, axis=0)
    fill_table(table, FIELDS * HALF, 0, edges)
    fill_table(table, FIELDS * HALF, 1, jnp.zeros_like(edges))
    fill_words(words, scales, lambda f: rim[f])

    @pl.loop(0, blocks, unroll=8)
    def _(number):
        found = gather(table, words, scales, RIM, rim_cells, shares, number)
        for f in range(FIELDS):
            values[number, f : f + 1, :] = found[f] + part[number, f : f + 1, :]


def place_kernel(incoming, near, rim, lines, pick, taken, updated, high, low):
    blocks = incoming.shape[0]
    width_y = near.shape[2]
    for number in range(blocks):
        span = slice(number * LANES, (number + 1) * LANES)
        value = incoming[number]
        upper = value.astype(jnp.bfloat16).astype(jnp.float32)
        lower = value - upper
        for f in range(FIELDS):
            for part, target in ((upper, high), (lower, low)):
                wide = jnp.broadcast_to(part[f : f + 1], (16, LANES)).astype(jnp.bfloat16)
                for first in range(0, INNER, 16):
                    target[f * INNER + first : f * INNER + first + 16, span] = (
                        lines[first : first + 16, span] * wide
                    )
    placed = jnp.dot(high[...], pick[...], preferred_element_type=jnp.float32)
    placed = placed + jnp.dot(low[...], pick[...], preferred_element_type=jnp.float32)
    for plane in range(4):
        rows = (plane % 2) * width_y
        lanes = slice((plane // 2) * LANES, (plane // 2 + 1) * LANES)
        free = taken[rows : rows + width_y, lanes] < 0.5
        for f in range(FIELDS):
            value = placed[f * INNER + rows : f * INNER + rows + width_y, lanes]
            if plane in (0, 3):
                at_row = 0 if plane == 0 else width_y
                updated[plane, f] = jnp.where(free, rim[f, at_row : at_row + width_y], value)
                continue
            updated[plane, f] = jnp.where(free, near[plane - 1, f], value)
            for at_row, y_line in ((63 + plane, 0), (65 + plane, width_y - 1)):
                one = slice(y_line, y_line + 1)
                updated[plane, f, one] = jnp.where(
                    free[one], rim[f, at_row : at_row + 1], value[one]
                )


def halo(ends, axis, head, tail):
    return (
        lax.ppermute(tail, axis, [(i, i + 1) for i in range(ends)]),
        lax.ppermute(head, axis, [(i + 1, i) for i in range(ends)]),
    )


def shards(
    flow_state,
    source,
    diag_scale,
    flux_jac,
    line_coupling,
    block_inverse,
    active_order,
    active_units,
    donor_cells,
    donor_weights,
    receptor_cells,
):
    f32, i32 = jnp.float32, jnp.int32
    vmem = pl.BlockSpec(memory_space=pltpu.VMEM)
    smem = pl.BlockSpec(memory_space=pltpu.SMEM)
    like = jax.ShapeDtypeStruct
    params = pltpu.CompilerParams(vmem_limit_bytes=32 << 20)
    flow = jnp.transpose(flow_state, (0, 2, 1, 3))
    source = jnp.transpose(source, (0, 2, 1, 3))
    jac = jnp.transpose(flux_jac, (1, 0, 2))
    coupling = jnp.transpose(line_coupling, (1, 0, 2))
    width_x, fields, width_y, length = flow.shape
    cells = donor_cells.reshape(donor_cells.shape[2:])
    weights = donor_weights.reshape(donor_weights.shape[2:])
    receptor = receptor_cells.reshape(receptor_cells.shape[2:])
    blocks = receptor.shape[0]

    outside = pl.BlockSpec(memory_space=pltpu.HBM)
    raw = [
        array if array is active_units else pltpu.with_memory_space_constraint(array, pltpu.HBM)
        for array in (
            jac, coupling, block_inverse, active_units, active_order.reshape(1, LANES),
            receptor, flow, source, diag_scale, cells, weights,
        )
    ]
    *edges, flow, source, diag, cells, weights, live, lines, pick, taken, matrices = pl.pallas_call(
        load_kernel,
        out_shape=[like((fields, width_y, length), f32)] * 2
        + [like((fields, width_x, length), f32)] * 2
        + [like(array.shape, array.dtype) for array in raw[6:]]
        + [
            like((LANES, LANES), f32),
            like((INNER, blocks * LANES), jnp.bfloat16),
            like((blocks * LANES, 2 * LANES), jnp.bfloat16),
            like((INNER, 2 * LANES), f32),
            like((8, fields, fields), f32),
        ],
        in_specs=[outside] * 11,
        out_specs=[vmem] * 13 + [smem],
        scratch_shapes=[
            pltpu.SMEM(jac.shape, f32),
            pltpu.SMEM(coupling.shape, f32),
            pltpu.SMEM(block_inverse.shape, f32),
            pltpu.SMEM(active_units.shape, i32),
            pltpu.VMEM((1, LANES), i32),
            pltpu.VMEM(receptor.shape, i32),
            pltpu.SemaphoreType.DMA((13,)),
        ],
        compiler_params=params,
        name="load_block",
    )(*raw)
    x_head, x_tail, y_head, y_tail = edges
    x_prev, x_next = halo(lax.axis_size("blk") - 1, "blk", x_head, x_tail)
    y_prev, y_next = halo(lax.axis_size("bal") - 1, "bal", y_head, y_tail)
    part, near, *rest = pl.pallas_call(
        inner_kernel,
        out_shape=[
            like((blocks, fields, length), f32),
            like((2, fields, width_y, length), f32),
            like((fields, RIM, length), f32),
            like((RIM, length), f32),
            like((RIM, length), f32),
            like((fields, RIM, length), f32),
            like(cells.shape, i32),
            like(cells.shape, f32),
        ],
        in_specs=[smem] + [vmem] * 6,
        out_specs=[vmem] * 8,
        scratch_shapes=[
            pltpu.VMEM(cells.shape, i32),
            pltpu.VMEM(cells.shape, f32),
            pltpu.VMEM((fields * HALF, 4 * LANES), jnp.bfloat16),
            pltpu.VMEM((4, INNER, LANES), i32),
            pltpu.VMEM((fields, 8, LANES), f32),
        ],
        cost_estimate=pl.CostEstimate(
            flops=10**10, bytes_accessed=3 * 10**6, transcendentals=0
        ),
        compiler_params=params,
        name="inner_lines",
    )(
        matrices, flow, source, diag, live, cells, weights,
    )
    values, rim = pl.pallas_call(
        rim_kernel,
        out_shape=[
            like((blocks, fields, length), f32),
            like((fields, RIM, length), f32),
        ],
        in_specs=[smem] + [vmem] * 11,
        out_specs=[vmem] * 2,
        scratch_shapes=[
            pltpu.VMEM((fields, RIM, length), f32),
            pltpu.VMEM((fields * (RIM - HALF), 4 * LANES), jnp.bfloat16),
            pltpu.VMEM((4, RIM, LANES), i32),
            pltpu.VMEM((fields, 8, LANES), f32),
        ],
        compiler_params=params,
        name="rim_lines",
    )(matrices, x_prev, x_next, y_prev, y_next, part, *rest)
    incoming = lax.all_to_all(values, "blk", split_axis=0, concat_axis=0, tiled=True)
    updated = pl.pallas_call(
        place_kernel,
        out_shape=like(flow.shape, f32),
        in_specs=[vmem] * 6,
        out_specs=vmem,
        scratch_shapes=[pltpu.VMEM((fields * INNER, blocks * LANES), jnp.bfloat16)] * 2,
        compiler_params=params,
        name="place_receptors",
    )(incoming, near, rim, lines, pick, taken)
    return jnp.transpose(updated, (0, 2, 1, 3))


def solution(mesh):
    placed = (
        P("blk", "bal", None, None),
        P("blk", "bal", None, None),
        P("blk", "bal", None),
        P(),
        P(),
        P(),
        P("blk", "bal", None),
        P("blk", "bal"),
        P("blk", "bal", None, None, None),
        P("blk", "bal", None, None, None),
        P("blk", "bal", None, None),
    )
    return jax.shard_map(
        shards, mesh=mesh, in_specs=placed, out_specs=P("blk", "bal", None, None), check_vma=False
    )
```

```python
import functools

import jax
import jax.numpy as jnp
from jax import lax
from jax.experimental import pallas as pl
from jax.experimental.pallas import tpu as pltpu
from jax.sharding import PartitionSpec as P

SWEEPS = 4
FIELDS = 6
DONORS = 8
LANES = 128
INNER = 64
RIM = 72
HALF = 32
BY_MATRIX = 4
STEPS = 1048000.0


def entry(number, f, g):
    row = (number * FIELDS + f) * FIELDS + g
    return slice(row, row + 1)


def apply(matrix, values):
    out = []
    for f in range(FIELDS):
        total = matrix(f, 0) * values[0]
        for g in range(1, FIELDS):
            total = total + matrix(f, g) * values[g]
        out.append(total)
    return out


def solve(residual, scale_inv, matrices):
    lane = lax.broadcasted_iota(jnp.int32, residual[0].shape, 1)
    first, last = lane == 0, lane == LANES - 1
    base = apply(lambda f, g: matrices[entry(3, f, g)], residual)
    base = [value * scale_inv for value in base]
    correction = base
    for _ in range(SWEEPS - 1):
        total = [None] * FIELDS
        for g in range(FIELDS):
            down = jnp.where(first, 0.0, pltpu.roll(correction[g], 1, 1))
            up = jnp.where(last, 0.0, pltpu.roll(correction[g], LANES - 1, 1))
            for f in range(FIELDS):
                term = matrices[entry(1, f, g)] * down + matrices[entry(2, f, g)] * up
                total[f] = term if g == 0 else total[f] + term
        correction = [base[f] - scale_inv * total[f] for f in range(FIELDS)]
    return correction


def fill_table(table, first, half, values):
    high = values.astype(jnp.bfloat16)
    low = (values - high.astype(jnp.float32)).astype(jnp.bfloat16)
    rows = slice(first, first + values.shape[0])
    table[rows, half * LANES : (half + 1) * LANES] = high
    table[rows, (half + 2) * LANES : (half + 3) * LANES] = low


def fill_words(words, scales, corrected):
    whole = []
    for f in range(FIELDS):
        largest = jnp.max(jnp.max(jnp.abs(corrected(f)), axis=0, keepdims=True), axis=1, keepdims=True)
        scale = jnp.broadcast_to(jnp.maximum(largest, 1e-30), (8, LANES))
        scales[f] = scale * (1.0 / (STEPS * 2048.0))
        factor = (STEPS / scale)[0:1]
        whole.append(jnp.round(corrected(f) * factor).astype(jnp.int32))
    parts = []
    for f in (4, 5):
        upper = (whole[f] + 512) >> 10
        parts += [upper, whole[f] - (upper << 10)]
    for word in range(4):
        words[word] = (whole[word] << 11) + parts[word]


def gather_by_lane(words, rows, cell, share, total):
    below = lax.broadcasted_iota(jnp.int32, (8, LANES), 0)
    cell = jnp.broadcast_to(cell, (8, LANES))
    pos = cell & (LANES - 1)
    line = (cell >> 7) - below
    share = jnp.where((line & 7) == 0, jnp.broadcast_to(share, (8, LANES)), 0.0)
    hit = [None] * 4
    for first in range(0, rows, 8):
        chosen = line == first
        for word in range(4):
            found = jnp.take_along_axis(
                words[word, first : first + 8], pos, axis=1, mode="promise_in_bounds"
            )
            hit[word] = found if first == 0 else jnp.where(chosen, found, hit[word])
    low = [(value << 21).astype(jnp.float32) for value in hit]
    found = [value.astype(jnp.float32) for value in hit]
    found += [low[0] + low[1] * (1.0 / 1024), low[2] + low[3] * (1.0 / 1024)]
    return [
        value * share if total is None else total[f] + value * share
        for f, value in enumerate(found)
    ]


def small(numbers):
    return numbers.astype(jnp.float32).astype(jnp.bfloat16)


def gather(table, words, scales, rows, cells, shares, number):
    at_cell = small(lax.broadcasted_iota(jnp.int32, (2 * LANES, 2 * LANES), 0))
    at_line = lax.broadcasted_iota(jnp.int32, (rows - HALF, 2 * LANES), 0)
    one, zero = jnp.bfloat16(1), jnp.bfloat16(0)
    extra = rows - 2 * HALF
    total = [None] * FIELDS
    for k in range(0, BY_MATRIX, 2):
        cell = jnp.concatenate([cells[k + i, pl.ds(number, 1), :] for i in (0, 1)], axis=1)
        share = jnp.concatenate([shares[k + i, pl.ds(number, 1), :] for i in (0, 1)], axis=1)
        column = ((cell >> 5) & LANES) + (cell & (LANES - 1))
        line = ((cell >> 7) & (HALF - 1)) + ((cell >> 8) & HALF)
        pick = jnp.where(at_cell == small(column), one, zero)
        found = jnp.dot(
            table[...], jnp.concatenate([pick, pick], axis=0), preferred_element_type=jnp.float32
        )
        weight = jnp.where(at_line == line, share, 0.0)
        for f in range(FIELDS):
            part = found[f * HALF : (f + 1) * HALF] * weight[:HALF]
            part = jnp.sum(part.reshape(HALF // 8, 8, 2 * LANES), axis=0)
            if extra:
                first = FIELDS * HALF + f * extra
                part = part + found[first : first + extra] * weight[HALF:]
            total[f] = part if k == 0 else total[f] + part
    by_lane = None
    for k in range(BY_MATRIX, DONORS):
        by_lane = gather_by_lane(
            words, rows, cells[k, pl.ds(number, 1), :], shares[k, pl.ds(number, 1), :], by_lane
        )
    return [
        jnp.sum(
            value[:, :LANES] + value[:, LANES:] + by_lane[f] * scales[f], axis=0, keepdims=True
        )
        for f, value in enumerate(total)
    ]


def prepare(receptor, lines, pick, taken):
    at_line = lax.broadcasted_iota(jnp.int32, (INNER, LANES), 0)
    at_cell = lax.broadcasted_iota(jnp.int32, (LANES, LANES), 1)
    for number in range(receptor.shape[0]):
        cell = receptor[number : number + 1, :]
        line = cell >> 7
        where = ((line >> 6) << 7) + (cell & (LANES - 1))
        span = slice(number * LANES, (number + 1) * LANES)
        lines[:, span] = jnp.where(at_line == (line & (INNER - 1)), 1.0, 0.0).astype(jnp.bfloat16)
        where = jnp.transpose(jnp.broadcast_to(where, (LANES, LANES)))
        for half in (0, 1):
            pick[span, half * LANES : (half + 1) * LANES] = jnp.where(
                at_cell + half * LANES == where, 1.0, 0.0
            ).astype(jnp.bfloat16)
    taken[...] = jnp.dot(lines[...], pick[...], preferred_element_type=jnp.float32)


def load_kernel(
    jac_in, coupling_in, inverse_in, units_in, order_in, receptor_in,
    flow_in, source_in, diag_in, cells_in, weights_in,
    x_head, x_tail, y_head, y_tail, flow, source, diag, cells, weights,
    live, lines, pick, taken, matrices,
    jac, coupling, inverse, units, order, receptor, done,
):
    width_x, _, width_y, _ = flow.shape
    copies = [
        pltpu.make_async_copy(origin, target, done.at[number])
        for number, (origin, target) in enumerate(
            (
                (jac_in, jac),
                (coupling_in, coupling),
                (inverse_in, inverse),
                (units_in, units),
                (order_in, order),
                (receptor_in, receptor),
                (flow_in, flow),
                (flow_in.at[0], x_head),
                (flow_in.at[width_x - 1], x_tail),
                (source_in, source),
                (diag_in, diag),
                (cells_in, cells),
                (weights_in, weights),
            )
        )
    ]
    for copy in copies:
        copy.start()
    for copy in copies[:6]:
        copy.wait()
    for f in range(FIELDS):
        for g in range(FIELDS):
            values = [jac[f, 0, g] + jac[f, 1, g] + jac[f, 2, g] + jac[f, 3, g]]
            for side in (0, 1):
                total = inverse[f, 0] * coupling[0, side, g]
                for h in range(1, FIELDS):
                    total = total + inverse[f, h] * coupling[h, side, g]
                values.append(total)
            values.append(inverse[f, g])
            values += [jac[f, side, g] for side in range(4)]
            for number, value in enumerate(values):
                matrices[entry(number, f, g)] = jnp.full((1, LANES), value, jnp.float32)
    line = lax.broadcasted_iota(jnp.int32, (LANES, LANES), 0)
    place = lax.broadcasted_iota(jnp.int32, (LANES, LANES), 1)
    hit = (line == order[...]) & (place < units[0, 0] * 32)
    live[...] = jnp.broadcast_to(
        jnp.max(jnp.where(hit, 1.0, 0.0), axis=1, keepdims=True), (LANES, LANES)
    )
    prepare(receptor, lines, pick, taken)
    copies[6].wait()
    for f in range(FIELDS):
        for x in range(width_x):
            y_head[f, x : x + 1] = flow[x, f, 0:1]
            y_tail[f, x : x + 1] = flow[x, f, width_y - 1 : width_y]
    for copy in copies[7:]:
        copy.wait()


def inner_kernel(
    matrices, flow, source, diag, live, cells, weights,
    values, near, rim_residual, rim_scale, rim_live, rim_flow, rim_cells, rim_shares,
    inner_cells, inner_shares, table, words, scales,
):
    width_y = flow.shape[2]
    blocks = cells.shape[1]
    row = lax.broadcasted_iota(jnp.int32, (width_y, LANES), 0)

    cell = cells[...]
    at = cell >> 7
    x, y = at >> 5, at & 31
    middle = (x == 1) | (x == 2)
    edge = middle & ((y == 0) | (y == width_y - 1))
    pos = cell & (LANES - 1)
    inner = middle & ~edge
    inner_cells[...] = (((at - 32) & (INNER - 1)) << 7) + pos
    on_edge = 64 + (x - 1) + jnp.where(y == 0, 0, 2)
    on_rim = jnp.where(x == 0, at, (at - 64) & 63)
    rim_cells[...] = (jnp.where(edge, on_edge, on_rim) << 7) + pos
    weight = weights[...]
    share = weight / jnp.sum(weight, axis=0, keepdims=True)
    inner_shares[...] = jnp.where(inner, share, 0.0)
    rim_shares[...] = jnp.where(inner, 0.0, share)

    def residual_of(plane):
        total = [source[plane, f] for f in range(FIELDS)]
        for g in range(FIELDS):
            here = flow[plane, g]
            left = flow[plane - 1, g] if plane > 0 else None
            right = flow[plane + 1, g] if plane < 3 else None
            before = jnp.where(row == 0, 0.0, pltpu.roll(here, 1, 0))
            after = jnp.where(row == width_y - 1, 0.0, pltpu.roll(here, width_y - 1, 0))
            for f in range(FIELDS):
                value = total[f] - matrices[entry(0, f, g)] * here
                if left is not None:
                    value = value + matrices[entry(4, f, g)] * left
                if right is not None:
                    value = value + matrices[entry(5, f, g)] * right
                total[f] = value + matrices[entry(6, f, g)] * before + matrices[entry(7, f, g)] * after
        return total

    for number, plane in enumerate((0, 3)):
        residual = residual_of(plane)
        rows = slice(number * width_y, (number + 1) * width_y)
        for f in range(FIELDS):
            rim_residual[f, rows] = residual[f]
            rim_flow[f, rows] = flow[plane, f]
        rim_scale[rows] = 1.0 / diag[plane]
        rim_live[rows] = live[plane * width_y : (plane + 1) * width_y]
    rim_scale[RIM - 8 : RIM] = jnp.ones((8, LANES), jnp.float32)
    rim_live[RIM - 8 : RIM] = jnp.zeros((8, LANES), jnp.float32)
    for f in range(FIELDS):
        rim_residual[f, RIM - 8 : RIM] = jnp.zeros((8, LANES), jnp.float32)
        rim_flow[f, RIM - 8 : RIM] = jnp.zeros((8, LANES), jnp.float32)
    for number, plane in enumerate((1, 2)):
        residual = residual_of(plane)
        scale = 1.0 / diag[plane]
        alive = live[plane * width_y : (plane + 1) * width_y]
        for at_row, y_line in ((64 + number, 0), (66 + number, width_y - 1)):
            for f in range(FIELDS):
                rim_residual[f, at_row : at_row + 1] = residual[f][y_line : y_line + 1]
                rim_flow[f, at_row : at_row + 1] = flow[plane, f, y_line : y_line + 1]
            rim_scale[at_row : at_row + 1] = scale[y_line : y_line + 1]
            rim_live[at_row : at_row + 1] = alive[y_line : y_line + 1]
        correction = solve(residual, scale, matrices)
        for f in range(FIELDS):
            corrected = flow[plane, f] + jnp.where(alive > 0.5, correction[f], 0.0)
            near[number, f] = corrected
            fill_table(table, f * HALF, number, corrected)

    fill_words(
        words, scales, lambda f: jnp.concatenate([near[0, f], near[1, f]], axis=0)
    )

    @pl.loop(0, blocks, unroll=8)
    def _(number):
        found = gather(table, words, scales, INNER, inner_cells, inner_shares, number)
        for f in range(FIELDS):
            values[number, f : f + 1, :] = found[f]


def rim_kernel(
    matrices, x_prev, x_next, y_prev, y_next,
    part, rim_residual, rim_scale, rim_live, rim_flow, rim_cells, shares,
    values, rim, residual, table, words, scales,
):
    width_y = x_prev.shape[1]
    blocks = rim_cells.shape[1]
    for number, (side, halo) in enumerate(((0, x_prev), (1, x_next))):
        rows = slice(number * width_y, (number + 1) * width_y)
        added = apply(lambda f, g: matrices[entry(4 + side, f, g)], [halo[g] for g in range(FIELDS)])
        for f in range(FIELDS):
            residual[f, rows] = rim_residual[f, rows] + added[f]
    for number, (side, halo) in enumerate(((2, y_prev), (3, y_next))):
        added = apply(lambda f, g: matrices[entry(4 + side, f, g)], [halo[g] for g in range(FIELDS)])
        for f in range(FIELDS):
            at_row = 64 + 2 * number
            residual[f, at_row : at_row + 2] = (
                rim_residual[f, at_row : at_row + 2] + added[f][1:3]
            )
            for at_row, x in ((number * (width_y - 1), 0), (width_y + number * (width_y - 1), 3)):
                residual[f, at_row : at_row + 1] = (
                    residual[f, at_row : at_row + 1] + added[f][x : x + 1]
                )
    for f in range(FIELDS):
        residual[f, RIM - 4 : RIM] = jnp.zeros((4, LANES), jnp.float32)
    edges = []
    for half, rows in enumerate((slice(0, 32), slice(32, 64), slice(64, RIM))):
        correction = solve(
            [residual[f, rows] for f in range(FIELDS)], rim_scale[rows], matrices
        )
        alive = rim_live[rows] > 0.5
        for f in range(FIELDS):
            corrected = rim_flow[f, rows] + jnp.where(alive, correction[f], 0.0)
            rim[f, rows] = corrected
            if half < 2:
                fill_table(table, f * HALF, half, corrected)
            else:
                edges.append(corrected)
    edges = jnp.concatenate(edges, axis=0)
    fill_table(table, FIELDS * HALF, 0, edges)
    fill_table(table, FIELDS * HALF, 1, jnp.zeros_like(edges))
    fill_words(words, scales, lambda f: rim[f])

    @pl.loop(0, blocks, unroll=8)
    def _(number):
        found = gather(table, words, scales, RIM, rim_cells, shares, number)
        for f in range(FIELDS):
            values[number, f : f + 1, :] = found[f] + part[number, f : f + 1, :]


def place_kernel(incoming, near, rim, lines, pick, taken, updated, high, low):
    blocks = incoming.shape[0]
    width_y = near.shape[2]
    for number in range(blocks):
        span = slice(number * LANES, (number + 1) * LANES)
        value = incoming[number]
        upper = value.astype(jnp.bfloat16).astype(jnp.float32)
        lower = value - upper
        for f in range(FIELDS):
            for part, target in ((upper, high), (lower, low)):
                wide = jnp.broadcast_to(part[f : f + 1], (16, LANES)).astype(jnp.bfloat16)
                for first in range(0, INNER, 16):
                    target[f * INNER + first : f * INNER + first + 16, span] = (
                        lines[first : first + 16, span] * wide
                    )
    placed = jnp.dot(high[...], pick[...], preferred_element_type=jnp.float32)
    placed = placed + jnp.dot(low[...], pick[...], preferred_element_type=jnp.float32)
    for plane in range(4):
        rows = (plane % 2) * width_y
        lanes = slice((plane // 2) * LANES, (plane // 2 + 1) * LANES)
        free = taken[rows : rows + width_y, lanes] < 0.5
        for f in range(FIELDS):
            value = placed[f * INNER + rows : f * INNER + rows + width_y, lanes]
            if plane in (0, 3):
                at_row = 0 if plane == 0 else width_y
                updated[plane, f] = jnp.where(free, rim[f, at_row : at_row + width_y], value)
                continue
            updated[plane, f] = jnp.where(free, near[plane - 1, f], value)
            for at_row, y_line in ((63 + plane, 0), (65 + plane, width_y - 1)):
                one = slice(y_line, y_line + 1)
                updated[plane, f, one] = jnp.where(
                    free[one], rim[f, at_row : at_row + 1], value[one]
                )


def halo(ends, axis, head, tail):
    return (
        lax.ppermute(tail, axis, [(i, i + 1) for i in range(ends)]),
        lax.ppermute(head, axis, [(i + 1, i) for i in range(ends)]),
    )


def shards(
    flow_state,
    source,
    diag_scale,
    flux_jac,
    line_coupling,
    block_inverse,
    active_order,
    active_units,
    donor_cells,
    donor_weights,
    receptor_cells,
):
    f32, i32 = jnp.float32, jnp.int32
    vmem = pl.BlockSpec(memory_space=pltpu.VMEM)
    like = jax.ShapeDtypeStruct
    params = pltpu.CompilerParams(vmem_limit_bytes=32 << 20)
    flow = jnp.transpose(flow_state, (0, 2, 1, 3))
    source = jnp.transpose(source, (0, 2, 1, 3))
    jac = jnp.transpose(flux_jac, (1, 0, 2))
    coupling = jnp.transpose(line_coupling, (1, 0, 2))
    width_x, fields, width_y, length = flow.shape
    cells = donor_cells.reshape(donor_cells.shape[2:])
    weights = donor_weights.reshape(donor_weights.shape[2:])
    receptor = receptor_cells.reshape(receptor_cells.shape[2:])
    blocks = receptor.shape[0]

    outside = pl.BlockSpec(memory_space=pltpu.HBM)
    raw = [
        array if array is active_units else pltpu.with_memory_space_constraint(array, pltpu.HBM)
        for array in (
            jac, coupling, block_inverse, active_units, active_order.reshape(1, LANES),
            receptor, flow, source, diag_scale, cells, weights,
        )
    ]
    *edges, flow, source, diag, cells, weights, live, lines, pick, taken, matrices = pl.pallas_call(
        load_kernel,
        out_shape=[like((fields, width_y, length), f32)] * 2
        + [like((fields, width_x, length), f32)] * 2
        + [like(array.shape, array.dtype) for array in raw[6:]]
        + [
            like((LANES, LANES), f32),
            like((INNER, blocks * LANES), jnp.bfloat16),
            like((blocks * LANES, 2 * LANES), jnp.bfloat16),
            like((INNER, 2 * LANES), f32),
            like((8 * fields * fields, length), f32),
        ],
        in_specs=[outside] * 11,
        out_specs=[vmem] * 14,
        scratch_shapes=[
            pltpu.SMEM(jac.shape, f32),
            pltpu.SMEM(coupling.shape, f32),
            pltpu.SMEM(block_inverse.shape, f32),
            pltpu.SMEM(active_units.shape, i32),
            pltpu.VMEM((1, LANES), i32),
            pltpu.VMEM(receptor.shape, i32),
            pltpu.SemaphoreType.DMA((13,)),
        ],
        compiler_params=params,
        name="load_block",
    )(*raw)
    x_head, x_tail, y_head, y_tail = edges
    x_prev, x_next = halo(lax.axis_size("blk") - 1, "blk", x_head, x_tail)
    y_prev, y_next = halo(lax.axis_size("bal") - 1, "bal", y_head, y_tail)
    part, near, *rest = pl.pallas_call(
        inner_kernel,
        out_shape=[
            like((blocks, fields, length), f32),
            like((2, fields, width_y, length), f32),
            like((fields, RIM, length), f32),
            like((RIM, length), f32),
            like((RIM, length), f32),
            like((fields, RIM, length), f32),
            like(cells.shape, i32),
            like(cells.shape, f32),
        ],
        in_specs=[vmem] * 7,
        out_specs=[vmem] * 8,
        scratch_shapes=[
            pltpu.VMEM(cells.shape, i32),
            pltpu.VMEM(cells.shape, f32),
            pltpu.VMEM((fields * HALF, 4 * LANES), jnp.bfloat16),
            pltpu.VMEM((4, INNER, LANES), i32),
            pltpu.VMEM((fields, 8, LANES), f32),
        ],
        cost_estimate=pl.CostEstimate(
            flops=10**10, bytes_accessed=3 * 10**6, transcendentals=0
        ),
        compiler_params=params,
        name="inner_lines",
    )(
        matrices, flow, source, diag, live, cells, weights,
    )
    values, rim = pl.pallas_call(
        rim_kernel,
        out_shape=[
            like((blocks, fields, length), f32),
            like((fields, RIM, length), f32),
        ],
        in_specs=[vmem] * 12,
        out_specs=[vmem] * 2,
        scratch_shapes=[
            pltpu.VMEM((fields, RIM, length), f32),
            pltpu.VMEM((fields * (RIM - HALF), 4 * LANES), jnp.bfloat16),
            pltpu.VMEM((4, RIM, LANES), i32),
            pltpu.VMEM((fields, 8, LANES), f32),
        ],
        compiler_params=params,
        name="rim_lines",
    )(matrices, x_prev, x_next, y_prev, y_next, part, *rest)
    incoming = lax.all_to_all(values, "blk", split_axis=0, concat_axis=0, tiled=True)
    updated = pl.pallas_call(
        place_kernel,
        out_shape=like(flow.shape, f32),
        in_specs=[vmem] * 6,
        out_specs=vmem,
        scratch_shapes=[pltpu.VMEM((fields * INNER, blocks * LANES), jnp.bfloat16)] * 2,
        compiler_params=params,
        name="place_receptors",
    )(incoming, near, rim, lines, pick, taken)
    return jnp.transpose(updated, (0, 2, 1, 3))


def solution(mesh):
    placed = (
        P("blk", "bal", None, None),
        P("blk", "bal", None, None),
        P("blk", "bal", None),
        P(),
        P(),
        P(),
        P("blk", "bal", None),
        P("blk", "bal"),
        P("blk", "bal", None, None, None),
        P("blk", "bal", None, None, None),
        P("blk", "bal", None, None),
    )
    return jax.shard_map(
        shards, mesh=mesh, in_specs=placed, out_specs=P("blk", "bal", None, None), check_vma=False
    )
```

```python
import functools

import jax
import jax.numpy as jnp
from jax import lax
from jax.experimental import pallas as pl
from jax.experimental.pallas import tpu as pltpu
from jax.sharding import PartitionSpec as P

SWEEPS = 4
FIELDS = 6
DONORS = 8
LANES = 128
INNER = 64
RIM = 72
HALF = 32
BY_MATRIX = 4
STEPS = 1048000.0
PARTS = 8


def entry(number, f, g):
    row = (number * FIELDS + f) * FIELDS + g
    return slice(row, row + 1)


def apply(matrix, values):
    out = []
    for f in range(FIELDS):
        total = matrix(f, 0) * values[0]
        for g in range(1, FIELDS):
            total = total + matrix(f, g) * values[g]
        out.append(total)
    return out


def solve(residual, scale_inv, matrices):
    lane = lax.broadcasted_iota(jnp.int32, residual[0].shape, 1)
    first, last = lane == 0, lane == LANES - 1
    base = apply(lambda f, g: matrices[entry(3, f, g)], residual)
    base = [value * scale_inv for value in base]
    correction = base
    for _ in range(SWEEPS - 1):
        total = [None] * FIELDS
        for g in range(FIELDS):
            down = jnp.where(first, 0.0, pltpu.roll(correction[g], 1, 1))
            up = jnp.where(last, 0.0, pltpu.roll(correction[g], LANES - 1, 1))
            for f in range(FIELDS):
                term = matrices[entry(1, f, g)] * down + matrices[entry(2, f, g)] * up
                total[f] = term if g == 0 else total[f] + term
        correction = [base[f] - scale_inv * total[f] for f in range(FIELDS)]
    return correction


def fill_table(table, first, half, values):
    high = values.astype(jnp.bfloat16)
    low = (values - high.astype(jnp.float32)).astype(jnp.bfloat16)
    rows = slice(first, first + values.shape[0])
    table[rows, half * LANES : (half + 1) * LANES] = high
    table[rows, (half + 2) * LANES : (half + 3) * LANES] = low


def fill_words(words, scales, corrected):
    whole = []
    for f in range(FIELDS):
        largest = jnp.max(jnp.max(jnp.abs(corrected(f)), axis=0, keepdims=True), axis=1, keepdims=True)
        scale = jnp.broadcast_to(jnp.maximum(largest, 1e-30), (8, LANES))
        scales[f] = scale * (1.0 / (STEPS * 2048.0))
        factor = (STEPS / scale)[0:1]
        whole.append(jnp.round(corrected(f) * factor).astype(jnp.int32))
    parts = []
    for f in (4, 5):
        upper = (whole[f] + 512) >> 10
        parts += [upper, whole[f] - (upper << 10)]
    for word in range(4):
        words[word] = (whole[word] << 11) + parts[word]


def gather_by_lane(words, rows, cell, share, total):
    below = lax.broadcasted_iota(jnp.int32, (8, LANES), 0)
    cell = jnp.broadcast_to(cell, (8, LANES))
    pos = cell & (LANES - 1)
    line = (cell >> 7) - below
    share = jnp.where((line & 7) == 0, jnp.broadcast_to(share, (8, LANES)), 0.0)
    hit = [None] * 4
    for first in range(0, rows, 8):
        chosen = line == first
        for word in range(4):
            found = jnp.take_along_axis(
                words[word, first : first + 8], pos, axis=1, mode="promise_in_bounds"
            )
            hit[word] = found if first == 0 else jnp.where(chosen, found, hit[word])
    low = [(value << 21).astype(jnp.float32) for value in hit]
    found = [value.astype(jnp.float32) for value in hit]
    found += [low[0] + low[1] * (1.0 / 1024), low[2] + low[3] * (1.0 / 1024)]
    return [
        value * share if total is None else total[f] + value * share
        for f, value in enumerate(found)
    ]


def small(numbers):
    return numbers.astype(jnp.float32).astype(jnp.bfloat16)


def gather(table, words, scales, rows, cells, shares, number):
    at_cell = small(lax.broadcasted_iota(jnp.int32, (2 * LANES, 2 * LANES), 0))
    at_line = lax.broadcasted_iota(jnp.int32, (rows - HALF, 2 * LANES), 0)
    one, zero = jnp.bfloat16(1), jnp.bfloat16(0)
    extra = rows - 2 * HALF
    total = [None] * FIELDS
    for k in range(0, BY_MATRIX, 2):
        cell = jnp.concatenate([cells[k + i, pl.ds(number, 1), :] for i in (0, 1)], axis=1)
        share = jnp.concatenate([shares[k + i, pl.ds(number, 1), :] for i in (0, 1)], axis=1)
        column = ((cell >> 5) & LANES) + (cell & (LANES - 1))
        line = ((cell >> 7) & (HALF - 1)) + ((cell >> 8) & HALF)
        pick = jnp.where(at_cell == small(column), one, zero)
        found = jnp.dot(
            table[...], jnp.concatenate([pick, pick], axis=0), preferred_element_type=jnp.float32
        )
        weight = jnp.where(at_line == line, share, 0.0)
        for f in range(FIELDS):
            part = found[f * HALF : (f + 1) * HALF] * weight[:HALF]
            part = jnp.sum(part.reshape(HALF // 8, 8, 2 * LANES), axis=0)
            if extra:
                first = FIELDS * HALF + f * extra
                part = part + found[first : first + extra] * weight[HALF:]
            total[f] = part if k == 0 else total[f] + part
    by_lane = None
    for k in range(BY_MATRIX, DONORS):
        by_lane = gather_by_lane(
            words, rows, cells[k, pl.ds(number, 1), :], shares[k, pl.ds(number, 1), :], by_lane
        )
    return [
        jnp.sum(
            value[:, :LANES] + value[:, LANES:] + by_lane[f] * scales[f], axis=0, keepdims=True
        )
        for f, value in enumerate(total)
    ]


def prepare(receptor, lines, pick, taken):
    at_line = lax.broadcasted_iota(jnp.int32, (INNER, LANES), 0)
    at_cell = lax.broadcasted_iota(jnp.int32, (LANES, LANES), 1)
    for number in range(receptor.shape[0]):
        cell = receptor[number : number + 1, :]
        line = cell >> 7
        where = ((line >> 6) << 7) + (cell & (LANES - 1))
        span = slice(number * LANES, (number + 1) * LANES)
        lines[:, span] = jnp.where(at_line == (line & (INNER - 1)), 1.0, 0.0).astype(jnp.bfloat16)
        where = jnp.transpose(jnp.broadcast_to(where, (LANES, LANES)))
        for half in (0, 1):
            pick[span, half * LANES : (half + 1) * LANES] = jnp.where(
                at_cell + half * LANES == where, 1.0, 0.0
            ).astype(jnp.bfloat16)
    taken[...] = jnp.dot(lines[...], pick[...], preferred_element_type=jnp.float32)


def load_kernel(
    jac_in, coupling_in, inverse_in, units_in, order_in, receptor_in,
    flow_in, source_in, diag_in, cells_in, weights_in,
    x_head, x_tail, y_head, y_tail, flow, source, diag, cells, weights,
    live, lines, pick, taken, matrices,
    jac, coupling, inverse, units, order, receptor, done,
):
    width_x, _, width_y, _ = flow.shape
    copies = [
        pltpu.make_async_copy(origin, target, done.at[number])
        for number, (origin, target) in enumerate(
            (
                (jac_in, jac),
                (coupling_in, coupling),
                (inverse_in, inverse),
                (units_in, units),
                (order_in, order),
                (receptor_in, receptor),
                (flow_in, flow),
                (flow_in.at[0], x_head),
                (flow_in.at[width_x - 1], x_tail),
                (source_in, source),
                (diag_in, diag),
                (cells_in, cells),
                (weights_in, weights),
            )
        )
    ]
    for copy in copies:
        copy.start()
    for copy in copies[:6]:
        copy.wait()
    for f in range(FIELDS):
        for g in range(FIELDS):
            values = [jac[f, 0, g] + jac[f, 1, g] + jac[f, 2, g] + jac[f, 3, g]]
            for side in (0, 1):
                total = inverse[f, 0] * coupling[0, side, g]
                for h in range(1, FIELDS):
                    total = total + inverse[f, h] * coupling[h, side, g]
                values.append(total)
            values.append(inverse[f, g])
            values += [jac[f, side, g] for side in range(4)]
            for number, value in enumerate(values):
                matrices[entry(number, f, g)] = jnp.full((1, LANES), value, jnp.float32)
    line = lax.broadcasted_iota(jnp.int32, (LANES, LANES), 0)
    place = lax.broadcasted_iota(jnp.int32, (LANES, LANES), 1)
    hit = (line == order[...]) & (place < units[0, 0] * 32)
    live[...] = jnp.broadcast_to(
        jnp.max(jnp.where(hit, 1.0, 0.0), axis=1, keepdims=True), (LANES, LANES)
    )
    prepare(receptor, lines, pick, taken)
    copies[6].wait()
    for f in range(FIELDS):
        for x in range(width_x):
            y_head[f, x : x + 1] = flow[x, f, 0:1]
            y_tail[f, x : x + 1] = flow[x, f, width_y - 1 : width_y]
    for copy in copies[7:]:
        copy.wait()


def inner_kernel(
    matrices, flow, source, diag, live, cells, weights,
    values, near, rim_residual, rim_scale, rim_live, rim_flow, rim_cells, rim_shares,
    inner_cells, inner_shares, table, words, scales,
):
    width_y = flow.shape[2]
    blocks = cells.shape[1]
    row = lax.broadcasted_iota(jnp.int32, (width_y, LANES), 0)

    cell = cells[...]
    at = cell >> 7
    x, y = at >> 5, at & 31
    middle = (x == 1) | (x == 2)
    edge = middle & ((y == 0) | (y == width_y - 1))
    pos = cell & (LANES - 1)
    inner = middle & ~edge
    inner_cells[...] = (((at - 32) & (INNER - 1)) << 7) + pos
    on_edge = 64 + (x - 1) + jnp.where(y == 0, 0, 2)
    on_rim = jnp.where(x == 0, at, (at - 64) & 63)
    rim_cells[...] = (jnp.where(edge, on_edge, on_rim) << 7) + pos
    weight = weights[...]
    share = weight / jnp.sum(weight, axis=0, keepdims=True)
    inner_shares[...] = jnp.where(inner, share, 0.0)
    rim_shares[...] = jnp.where(inner, 0.0, share)

    def residual_of(plane):
        total = [source[plane, f] for f in range(FIELDS)]
        for g in range(FIELDS):
            here = flow[plane, g]
            left = flow[plane - 1, g] if plane > 0 else None
            right = flow[plane + 1, g] if plane < 3 else None
            before = jnp.where(row == 0, 0.0, pltpu.roll(here, 1, 0))
            after = jnp.where(row == width_y - 1, 0.0, pltpu.roll(here, width_y - 1, 0))
            for f in range(FIELDS):
                value = total[f] - matrices[entry(0, f, g)] * here
                if left is not None:
                    value = value + matrices[entry(4, f, g)] * left
                if right is not None:
                    value = value + matrices[entry(5, f, g)] * right
                total[f] = value + matrices[entry(6, f, g)] * before + matrices[entry(7, f, g)] * after
        return total

    for number, plane in enumerate((0, 3)):
        residual = residual_of(plane)
        rows = slice(number * width_y, (number + 1) * width_y)
        for f in range(FIELDS):
            rim_residual[f, rows] = residual[f]
            rim_flow[f, rows] = flow[plane, f]
        rim_scale[rows] = 1.0 / diag[plane]
        rim_live[rows] = live[plane * width_y : (plane + 1) * width_y]
    rim_scale[RIM - 8 : RIM] = jnp.ones((8, LANES), jnp.float32)
    rim_live[RIM - 8 : RIM] = jnp.zeros((8, LANES), jnp.float32)
    for f in range(FIELDS):
        rim_residual[f, RIM - 8 : RIM] = jnp.zeros((8, LANES), jnp.float32)
        rim_flow[f, RIM - 8 : RIM] = jnp.zeros((8, LANES), jnp.float32)
    for number, plane in enumerate((1, 2)):
        residual = residual_of(plane)
        scale = 1.0 / diag[plane]
        alive = live[plane * width_y : (plane + 1) * width_y]
        for at_row, y_line in ((64 + number, 0), (66 + number, width_y - 1)):
            for f in range(FIELDS):
                rim_residual[f, at_row : at_row + 1] = residual[f][y_line : y_line + 1]
                rim_flow[f, at_row : at_row + 1] = flow[plane, f, y_line : y_line + 1]
            rim_scale[at_row : at_row + 1] = scale[y_line : y_line + 1]
            rim_live[at_row : at_row + 1] = alive[y_line : y_line + 1]
        correction = solve(residual, scale, matrices)
        for f in range(FIELDS):
            corrected = flow[plane, f] + jnp.where(alive > 0.5, correction[f], 0.0)
            near[number, f] = corrected
            fill_table(table, f * HALF, number, corrected)

    fill_words(
        words, scales, lambda f: jnp.concatenate([near[0, f], near[1, f]], axis=0)
    )

    @pl.loop(0, blocks, unroll=16)
    def _(number):
        found = gather(table, words, scales, INNER, inner_cells, inner_shares, number)
        for f in range(FIELDS):
            values[number, f : f + 1, :] = found[f]


def rim_kernel(
    matrices, x_prev, x_next, y_prev, y_next,
    part, rim_residual, rim_scale, rim_live, rim_flow, rim_cells, shares,
    values, rim, residual, table, words, scales,
):
    width_y = x_prev.shape[1]
    blocks = rim_cells.shape[1]
    for number, (side, halo) in enumerate(((0, x_prev), (1, x_next))):
        rows = slice(number * width_y, (number + 1) * width_y)
        added = apply(lambda f, g: matrices[entry(4 + side, f, g)], [halo[g] for g in range(FIELDS)])
        for f in range(FIELDS):
            residual[f, rows] = rim_residual[f, rows] + added[f]
    for number, (side, halo) in enumerate(((2, y_prev), (3, y_next))):
        added = apply(lambda f, g: matrices[entry(4 + side, f, g)], [halo[g] for g in range(FIELDS)])
        for f in range(FIELDS):
            at_row = 64 + 2 * number
            residual[f, at_row : at_row + 2] = (
                rim_residual[f, at_row : at_row + 2] + added[f][1:3]
            )
            for at_row, x in ((number * (width_y - 1), 0), (width_y + number * (width_y - 1), 3)):
                residual[f, at_row : at_row + 1] = (
                    residual[f, at_row : at_row + 1] + added[f][x : x + 1]
                )
    for f in range(FIELDS):
        residual[f, RIM - 4 : RIM] = jnp.zeros((4, LANES), jnp.float32)
    edges = []
    for half, rows in enumerate((slice(0, 32), slice(32, 64), slice(64, RIM))):
        correction = solve(
            [residual[f, rows] for f in range(FIELDS)], rim_scale[rows], matrices
        )
        alive = rim_live[rows] > 0.5
        for f in range(FIELDS):
            corrected = rim_flow[f, rows] + jnp.where(alive, correction[f], 0.0)
            rim[f, rows] = corrected
            if half < 2:
                fill_table(table, f * HALF, half, corrected)
            else:
                edges.append(corrected)
    edges = jnp.concatenate(edges, axis=0)
    fill_table(table, FIELDS * HALF, 0, edges)
    fill_table(table, FIELDS * HALF, 1, jnp.zeros_like(edges))
    fill_words(words, scales, lambda f: rim[f])

    @pl.loop(0, blocks, unroll=16)
    def _(number):
        found = gather(table, words, scales, RIM, rim_cells, shares, number)
        for f in range(FIELDS):
            values[number, f : f + 1, :] = found[f] + part[number, f : f + 1, :]


def place_kernel(incoming, near, rim, lines, pick, taken, updated, *parts):
    blocks = incoming.shape[0]
    width_y = near.shape[2]
    each = blocks // len(parts)
    placed = None
    for first_block, part in zip(range(0, blocks, each), parts):
        for number in range(first_block, first_block + each):
            span = slice(number * LANES, (number + 1) * LANES)
            column = (number - first_block) * LANES
            value = incoming[number]
            upper = value.astype(jnp.bfloat16).astype(jnp.float32)
            lower = value - upper
            for f in range(FIELDS):
                for values, start in ((upper, column), (lower, column + each * LANES)):
                    wide = jnp.broadcast_to(values[f : f + 1], (16, LANES)).astype(jnp.bfloat16)
                    for first in range(0, INNER, 16):
                        part[f * INNER + first : f * INNER + first + 16, start : start + LANES] = (
                            lines[first : first + 16, span] * wide
                        )
        chosen = pick[first_block * LANES : (first_block + each) * LANES]
        found = jnp.dot(
            part[...], jnp.concatenate([chosen, chosen], axis=0), preferred_element_type=jnp.float32
        )
        placed = found if placed is None else placed + found
    for plane in range(4):
        rows = (plane % 2) * width_y
        lanes = slice((plane // 2) * LANES, (plane // 2 + 1) * LANES)
        free = taken[rows : rows + width_y, lanes] < 0.5
        for f in range(FIELDS):
            value = placed[f * INNER + rows : f * INNER + rows + width_y, lanes]
            if plane in (0, 3):
                at_row = 0 if plane == 0 else width_y
                updated[plane, f] = jnp.where(free, rim[f, at_row : at_row + width_y], value)
                continue
            updated[plane, f] = jnp.where(free, near[plane - 1, f], value)
            for at_row, y_line in ((63 + plane, 0), (65 + plane, width_y - 1)):
                one = slice(y_line, y_line + 1)
                updated[plane, f, one] = jnp.where(
                    free[one], rim[f, at_row : at_row + 1], value[one]
                )


def halo(ends, axis, head, tail):
    return (
        lax.ppermute(tail, axis, [(i, i + 1) for i in range(ends)]),
        lax.ppermute(head, axis, [(i + 1, i) for i in range(ends)]),
    )


def shards(
    flow_state,
    source,
    diag_scale,
    flux_jac,
    line_coupling,
    block_inverse,
    active_order,
    active_units,
    donor_cells,
    donor_weights,
    receptor_cells,
):
    f32, i32 = jnp.float32, jnp.int32
    vmem = pl.BlockSpec(memory_space=pltpu.VMEM)
    like = jax.ShapeDtypeStruct
    params = pltpu.CompilerParams(vmem_limit_bytes=32 << 20)
    flow = jnp.transpose(flow_state, (0, 2, 1, 3))
    source = jnp.transpose(source, (0, 2, 1, 3))
    jac = jnp.transpose(flux_jac, (1, 0, 2))
    coupling = jnp.transpose(line_coupling, (1, 0, 2))
    width_x, fields, width_y, length = flow.shape
    cells = donor_cells.reshape(donor_cells.shape[2:])
    weights = donor_weights.reshape(donor_weights.shape[2:])
    receptor = receptor_cells.reshape(receptor_cells.shape[2:])
    blocks = receptor.shape[0]

    outside = pl.BlockSpec(memory_space=pltpu.HBM)
    raw = [
        array if array is active_units else pltpu.with_memory_space_constraint(array, pltpu.HBM)
        for array in (
            jac, coupling, block_inverse, active_units, active_order.reshape(1, LANES),
            receptor, flow, source, diag_scale, cells, weights,
        )
    ]
    *edges, flow, source, diag, cells, weights, live, lines, pick, taken, matrices = pl.pallas_call(
        load_kernel,
        out_shape=[like((fields, width_y, length), f32)] * 2
        + [like((fields, width_x, length), f32)] * 2
        + [like(array.shape, array.dtype) for array in raw[6:]]
        + [
            like((LANES, LANES), f32),
            like((INNER, blocks * LANES), jnp.bfloat16),
            like((blocks * LANES, 2 * LANES), jnp.bfloat16),
            like((INNER, 2 * LANES), f32),
            like((8 * fields * fields, length), f32),
        ],
        in_specs=[outside] * 11,
        out_specs=[vmem] * 14,
        scratch_shapes=[
            pltpu.SMEM(jac.shape, f32),
            pltpu.SMEM(coupling.shape, f32),
            pltpu.SMEM(block_inverse.shape, f32),
            pltpu.SMEM(active_units.shape, i32),
            pltpu.VMEM((1, LANES), i32),
            pltpu.VMEM(receptor.shape, i32),
            pltpu.SemaphoreType.DMA((13,)),
        ],
        compiler_params=params,
        name="load_block",
    )(*raw)
    x_head, x_tail, y_head, y_tail = edges
    x_prev, x_next = halo(lax.axis_size("blk") - 1, "blk", x_head, x_tail)
    y_prev, y_next = halo(lax.axis_size("bal") - 1, "bal", y_head, y_tail)
    part, near, *rest = pl.pallas_call(
        inner_kernel,
        out_shape=[
            like((blocks, fields, length), f32),
            like((2, fields, width_y, length), f32),
            like((fields, RIM, length), f32),
            like((RIM, length), f32),
            like((RIM, length), f32),
            like((fields, RIM, length), f32),
            like(cells.shape, i32),
            like(cells.shape, f32),
        ],
        in_specs=[vmem] * 7,
        out_specs=[vmem] * 8,
        scratch_shapes=[
            pltpu.VMEM(cells.shape, i32),
            pltpu.VMEM(cells.shape, f32),
            pltpu.VMEM((fields * HALF, 4 * LANES), jnp.bfloat16),
            pltpu.VMEM((4, INNER, LANES), i32),
            pltpu.VMEM((fields, 8, LANES), f32),
        ],
        cost_estimate=pl.CostEstimate(
            flops=10**10, bytes_accessed=3 * 10**6, transcendentals=0
        ),
        compiler_params=params,
        name="inner_lines",
    )(
        matrices, flow, source, diag, live, cells, weights,
    )
    values, rim = pl.pallas_call(
        rim_kernel,
        out_shape=[
            like((blocks, fields, length), f32),
            like((fields, RIM, length), f32),
        ],
        in_specs=[vmem] * 12,
        out_specs=[vmem] * 2,
        scratch_shapes=[
            pltpu.VMEM((fields, RIM, length), f32),
            pltpu.VMEM((fields * (RIM - HALF), 4 * LANES), jnp.bfloat16),
            pltpu.VMEM((4, RIM, LANES), i32),
            pltpu.VMEM((fields, 8, LANES), f32),
        ],
        compiler_params=params,
        name="rim_lines",
    )(matrices, x_prev, x_next, y_prev, y_next, part, *rest)
    incoming = lax.all_to_all(values, "blk", split_axis=0, concat_axis=0, tiled=True)
    updated = pl.pallas_call(
        place_kernel,
        out_shape=like(flow.shape, f32),
        in_specs=[vmem] * 6,
        out_specs=vmem,
        scratch_shapes=[pltpu.VMEM((fields * INNER, 2 * blocks * LANES // PARTS), jnp.bfloat16)] * PARTS,
        compiler_params=params,
        name="place_receptors",
    )(incoming, near, rim, lines, pick, taken)
    return jnp.transpose(updated, (0, 2, 1, 3))


def solution(mesh):
    placed = (
        P("blk", "bal", None, None),
        P("blk", "bal", None, None),
        P("blk", "bal", None),
        P(),
        P(),
        P(),
        P("blk", "bal", None),
        P("blk", "bal"),
        P("blk", "bal", None, None, None),
        P("blk", "bal", None, None, None),
        P("blk", "bal", None, None),
    )
    return jax.shard_map(
        shards, mesh=mesh, in_specs=placed, out_specs=P("blk", "bal", None, None), check_vma=False
    )
```

```python
import functools

import jax
import jax.numpy as jnp
from jax import lax
from jax.experimental import pallas as pl
from jax.experimental.pallas import tpu as pltpu
from jax.sharding import PartitionSpec as P

SWEEPS = 4
FIELDS = 6
DONORS = 8
LANES = 128
INNER = 64
RIM = 72
HALF = 32
BY_MATRIX = 4
STEPS = 1048000.0
PARTS = 8


def entry(number, f, g):
    row = (number * FIELDS + f) * FIELDS + g
    return slice(row, row + 1)


def apply(matrix, values):
    out = []
    for f in range(FIELDS):
        total = matrix(f, 0) * values[0]
        for g in range(1, FIELDS):
            total = total + matrix(f, g) * values[g]
        out.append(total)
    return out


def solve(residual, scale_inv, matrices):
    lane = lax.broadcasted_iota(jnp.int32, residual[0].shape, 1)
    first, last = lane == 0, lane == LANES - 1
    base = apply(lambda f, g: matrices[entry(3, f, g)], residual)
    base = [value * scale_inv for value in base]
    correction = base
    for _ in range(SWEEPS - 1):
        total = [None] * FIELDS
        for g in range(FIELDS):
            down = jnp.where(first, 0.0, pltpu.roll(correction[g], 1, 1))
            up = jnp.where(last, 0.0, pltpu.roll(correction[g], LANES - 1, 1))
            for f in range(FIELDS):
                term = matrices[entry(1, f, g)] * down + matrices[entry(2, f, g)] * up
                total[f] = term if g == 0 else total[f] + term
        correction = [base[f] - scale_inv * total[f] for f in range(FIELDS)]
    return correction


def fill_table(table, first, half, values):
    high = values.astype(jnp.bfloat16)
    low = (values - high.astype(jnp.float32)).astype(jnp.bfloat16)
    rows = slice(first, first + values.shape[0])
    table[rows, half * LANES : (half + 1) * LANES] = high
    table[rows, (half + 2) * LANES : (half + 3) * LANES] = low


def fill_words(words, scales, corrected):
    whole = []
    for f in range(FIELDS):
        largest = jnp.max(jnp.max(jnp.abs(corrected(f)), axis=0, keepdims=True), axis=1, keepdims=True)
        scale = jnp.broadcast_to(jnp.maximum(largest, 1e-30), (8, LANES))
        scales[f] = scale * (1.0 / (STEPS * 2048.0))
        factor = (STEPS / scale)[0:1]
        whole.append(jnp.round(corrected(f) * factor).astype(jnp.int32))
    parts = []
    for f in (4, 5):
        upper = (whole[f] + 512) >> 10
        parts += [upper, whole[f] - (upper << 10)]
    for word in range(4):
        words[word] = (whole[word] << 11) + parts[word]


def gather_by_lane(words, rows, cell, share, total):
    below = lax.broadcasted_iota(jnp.int32, (8, LANES), 0)
    cell = jnp.broadcast_to(cell, (8, LANES))
    pos = cell & (LANES - 1)
    line = (cell >> 7) - below
    share = jnp.where((line & 7) == 0, jnp.broadcast_to(share, (8, LANES)), 0.0)
    hit = [None] * 4
    for first in range(0, rows, 8):
        chosen = line == first
        for word in range(4):
            found = jnp.take_along_axis(
                words[word, first : first + 8], pos, axis=1, mode="promise_in_bounds"
            )
            hit[word] = found if first == 0 else jnp.where(chosen, found, hit[word])
    low = [(value << 21).astype(jnp.float32) for value in hit]
    found = [value.astype(jnp.float32) for value in hit]
    found += [low[0] + low[1] * (1.0 / 1024), low[2] + low[3] * (1.0 / 1024)]
    return [
        value * share if total is None else total[f] + value * share
        for f, value in enumerate(found)
    ]


def small(numbers):
    return numbers.astype(jnp.float32).astype(jnp.bfloat16)


def gather(table, words, scales, rows, cells, shares, number):
    at_cell = small(lax.broadcasted_iota(jnp.int32, (2 * LANES, 2 * LANES), 0))
    at_line = lax.broadcasted_iota(jnp.int32, (rows - HALF, 2 * LANES), 0)
    one, zero = jnp.bfloat16(1), jnp.bfloat16(0)
    extra = rows - 2 * HALF
    total = [None] * FIELDS
    for k in range(0, BY_MATRIX, 2):
        cell = jnp.concatenate([cells[k + i, pl.ds(number, 1), :] for i in (0, 1)], axis=1)
        share = jnp.concatenate([shares[k + i, pl.ds(number, 1), :] for i in (0, 1)], axis=1)
        column = ((cell >> 5) & LANES) + (cell & (LANES - 1))
        line = ((cell >> 7) & (HALF - 1)) + ((cell >> 8) & HALF)
        pick = jnp.where(at_cell == small(column), one, zero)
        found = jnp.dot(
            table[...], jnp.concatenate([pick, pick], axis=0), preferred_element_type=jnp.float32
        )
        weight = jnp.where(at_line == line, share, 0.0)
        for f in range(FIELDS):
            part = found[f * HALF : (f + 1) * HALF] * weight[:HALF]
            part = jnp.sum(part.reshape(HALF // 8, 8, 2 * LANES), axis=0)
            if extra:
                first = FIELDS * HALF + f * extra
                part = part + found[first : first + extra] * weight[HALF:]
            total[f] = part if k == 0 else total[f] + part
    by_lane = None
    for k in range(BY_MATRIX, DONORS):
        by_lane = gather_by_lane(
            words, rows, cells[k, pl.ds(number, 1), :], shares[k, pl.ds(number, 1), :], by_lane
        )
    return [
        jnp.sum(
            value[:, :LANES] + value[:, LANES:] + by_lane[f] * scales[f], axis=0, keepdims=True
        )
        for f, value in enumerate(total)
    ]


def prepare(receptor, lines, pick, taken):
    at_line = lax.broadcasted_iota(jnp.int32, (INNER, LANES), 0)
    at_cell = lax.broadcasted_iota(jnp.int32, (LANES, LANES), 1)
    for number in range(receptor.shape[0]):
        cell = receptor[number : number + 1, :]
        line = cell >> 7
        where = ((line >> 6) << 7) + (cell & (LANES - 1))
        span = slice(number * LANES, (number + 1) * LANES)
        lines[:, span] = jnp.where(at_line == (line & (INNER - 1)), 1.0, 0.0).astype(jnp.bfloat16)
        where = jnp.transpose(jnp.broadcast_to(where, (LANES, LANES)))
        for half in (0, 1):
            pick[span, half * LANES : (half + 1) * LANES] = jnp.where(
                at_cell + half * LANES == where, 1.0, 0.0
            ).astype(jnp.bfloat16)
    taken[...] = jnp.dot(lines[...], pick[...], preferred_element_type=jnp.float32)


def load_kernel(
    jac_in, coupling_in, inverse_in, units_in, order_in, receptor_in,
    flow_in, source_in, diag_in, cells_in, weights_in,
    x_even, x_odd, y_even, y_odd, flow, source, diag, cells, weights,
    live, lines, pick, taken, matrices,
    jac, coupling, inverse, units, order, receptor, done,
):
    width_x, _, width_y, _ = flow.shape
    copies = [
        pltpu.make_async_copy(origin, target, done.at[number])
        for number, (origin, target) in enumerate(
            (
                (jac_in, jac),
                (coupling_in, coupling),
                (inverse_in, inverse),
                (units_in, units),
                (order_in, order),
                (receptor_in, receptor),
                (flow_in, flow),
                (source_in, source),
                (diag_in, diag),
                (cells_in, cells),
                (weights_in, weights),
            )
        )
    ]
    for copy in copies:
        copy.start()
    for copy in copies[:6]:
        copy.wait()
    for f in range(FIELDS):
        for g in range(FIELDS):
            values = [jac[f, 0, g] + jac[f, 1, g] + jac[f, 2, g] + jac[f, 3, g]]
            for side in (0, 1):
                total = inverse[f, 0] * coupling[0, side, g]
                for h in range(1, FIELDS):
                    total = total + inverse[f, h] * coupling[h, side, g]
                values.append(total)
            values.append(inverse[f, g])
            values += [jac[f, side, g] for side in range(4)]
            for number, value in enumerate(values):
                matrices[entry(number, f, g)] = jnp.full((1, LANES), value, jnp.float32)
    line = lax.broadcasted_iota(jnp.int32, (LANES, LANES), 0)
    place = lax.broadcasted_iota(jnp.int32, (LANES, LANES), 1)
    hit = (line == order[...]) & (place < units[0, 0] * 32)
    live[...] = jnp.broadcast_to(
        jnp.max(jnp.where(hit, 1.0, 0.0), axis=1, keepdims=True), (LANES, LANES)
    )
    prepare(receptor, lines, pick, taken)
    copies[6].wait()
    upward = lax.rem(lax.axis_index("blk"), 2) == 0
    x_even[...] = jnp.where(upward, flow[width_x - 1], flow[0])
    x_odd[...] = jnp.where(upward, flow[0], flow[width_x - 1])
    upward = lax.rem(lax.axis_index("bal"), 2) == 0
    for f in range(FIELDS):
        for x in range(width_x):
            head, tail = flow[x, f, 0:1], flow[x, f, width_y - 1 : width_y]
            y_even[f, x : x + 1] = jnp.where(upward, tail, head)
            y_odd[f, x : x + 1] = jnp.where(upward, head, tail)
    for copy in copies[7:]:
        copy.wait()


def inner_kernel(
    matrices, flow, source, diag, live, cells, weights,
    values, near, rim_residual, rim_scale, rim_live, rim_flow, rim_cells, rim_shares,
    inner_cells, inner_shares, table, words, scales,
):
    width_y = flow.shape[2]
    blocks = cells.shape[1]
    row = lax.broadcasted_iota(jnp.int32, (width_y, LANES), 0)

    cell = cells[...]
    at = cell >> 7
    x, y = at >> 5, at & 31
    middle = (x == 1) | (x == 2)
    edge = middle & ((y == 0) | (y == width_y - 1))
    pos = cell & (LANES - 1)
    inner = middle & ~edge
    inner_cells[...] = (((at - 32) & (INNER - 1)) << 7) + pos
    on_edge = 64 + (x - 1) + jnp.where(y == 0, 0, 2)
    on_rim = jnp.where(x == 0, at, (at - 64) & 63)
    rim_cells[...] = (jnp.where(edge, on_edge, on_rim) << 7) + pos
    weight = weights[...]
    share = weight / jnp.sum(weight, axis=0, keepdims=True)
    inner_shares[...] = jnp.where(inner, share, 0.0)
    rim_shares[...] = jnp.where(inner, 0.0, share)

    def residual_of(plane):
        total = [source[plane, f] for f in range(FIELDS)]
        for g in range(FIELDS):
            here = flow[plane, g]
            left = flow[plane - 1, g] if plane > 0 else None
            right = flow[plane + 1, g] if plane < 3 else None
            before = jnp.where(row == 0, 0.0, pltpu.roll(here, 1, 0))
            after = jnp.where(row == width_y - 1, 0.0, pltpu.roll(here, width_y - 1, 0))
            for f in range(FIELDS):
                value = total[f] - matrices[entry(0, f, g)] * here
                if left is not None:
                    value = value + matrices[entry(4, f, g)] * left
                if right is not None:
                    value = value + matrices[entry(5, f, g)] * right
                total[f] = value + matrices[entry(6, f, g)] * before + matrices[entry(7, f, g)] * after
        return total

    for number, plane in enumerate((0, 3)):
        residual = residual_of(plane)
        rows = slice(number * width_y, (number + 1) * width_y)
        for f in range(FIELDS):
            rim_residual[f, rows] = residual[f]
            rim_flow[f, rows] = flow[plane, f]
        rim_scale[rows] = 1.0 / diag[plane]
        rim_live[rows] = live[plane * width_y : (plane + 1) * width_y]
    rim_scale[RIM - 8 : RIM] = jnp.ones((8, LANES), jnp.float32)
    rim_live[RIM - 8 : RIM] = jnp.zeros((8, LANES), jnp.float32)
    for f in range(FIELDS):
        rim_residual[f, RIM - 8 : RIM] = jnp.zeros((8, LANES), jnp.float32)
        rim_flow[f, RIM - 8 : RIM] = jnp.zeros((8, LANES), jnp.float32)
    for number, plane in enumerate((1, 2)):
        residual = residual_of(plane)
        scale = 1.0 / diag[plane]
        alive = live[plane * width_y : (plane + 1) * width_y]
        for at_row, y_line in ((64 + number, 0), (66 + number, width_y - 1)):
            for f in range(FIELDS):
                rim_residual[f, at_row : at_row + 1] = residual[f][y_line : y_line + 1]
                rim_flow[f, at_row : at_row + 1] = flow[plane, f, y_line : y_line + 1]
            rim_scale[at_row : at_row + 1] = scale[y_line : y_line + 1]
            rim_live[at_row : at_row + 1] = alive[y_line : y_line + 1]
        correction = solve(residual, scale, matrices)
        for f in range(FIELDS):
            corrected = flow[plane, f] + jnp.where(alive > 0.5, correction[f], 0.0)
            near[number, f] = corrected
            fill_table(table, f * HALF, number, corrected)

    fill_words(
        words, scales, lambda f: jnp.concatenate([near[0, f], near[1, f]], axis=0)
    )

    @pl.loop(0, blocks, unroll=16)
    def _(number):
        found = gather(table, words, scales, INNER, inner_cells, inner_shares, number)
        for f in range(FIELDS):
            values[number, f : f + 1, :] = found[f]


def rim_kernel(
    matrices, x_even, x_odd, y_even, y_odd,
    part, rim_residual, rim_scale, rim_live, rim_flow, rim_cells, shares,
    values, rim, residual, table, words, scales,
):
    width_y = x_even.shape[1]
    x_upward = lax.rem(lax.axis_index("blk"), 2) == 0
    y_upward = lax.rem(lax.axis_index("bal"), 2) == 0
    blocks = rim_cells.shape[1]
    for number, (side, halo) in enumerate(((0, (x_odd, x_even)), (1, (x_even, x_odd)))):
        rows = slice(number * width_y, (number + 1) * width_y)
        lines = [jnp.where(x_upward, halo[0][g], halo[1][g]) for g in range(FIELDS)]
        added = apply(lambda f, g: matrices[entry(4 + side, f, g)], lines)
        for f in range(FIELDS):
            residual[f, rows] = rim_residual[f, rows] + added[f]
    for number, (side, halo) in enumerate(((2, (y_odd, y_even)), (3, (y_even, y_odd)))):
        lines = [jnp.where(y_upward, halo[0][g], halo[1][g]) for g in range(FIELDS)]
        added = apply(lambda f, g: matrices[entry(4 + side, f, g)], lines)
        for f in range(FIELDS):
            at_row = 64 + 2 * number
            residual[f, at_row : at_row + 2] = (
                rim_residual[f, at_row : at_row + 2] + added[f][1:3]
            )
            for at_row, x in ((number * (width_y - 1), 0), (width_y + number * (width_y - 1), 3)):
                residual[f, at_row : at_row + 1] = (
                    residual[f, at_row : at_row + 1] + added[f][x : x + 1]
                )
    for f in range(FIELDS):
        residual[f, RIM - 4 : RIM] = jnp.zeros((4, LANES), jnp.float32)
    edges = []
    for half, rows in enumerate((slice(0, 32), slice(32, 64), slice(64, RIM))):
        correction = solve(
            [residual[f, rows] for f in range(FIELDS)], rim_scale[rows], matrices
        )
        alive = rim_live[rows] > 0.5
        for f in range(FIELDS):
            corrected = rim_flow[f, rows] + jnp.where(alive, correction[f], 0.0)
            rim[f, rows] = corrected
            if half < 2:
                fill_table(table, f * HALF, half, corrected)
            else:
                edges.append(corrected)
    edges = jnp.concatenate(edges, axis=0)
    fill_table(table, FIELDS * HALF, 0, edges)
    fill_table(table, FIELDS * HALF, 1, jnp.zeros_like(edges))
    fill_words(words, scales, lambda f: rim[f])

    @pl.loop(0, blocks, unroll=16)
    def _(number):
        found = gather(table, words, scales, RIM, rim_cells, shares, number)
        for f in range(FIELDS):
            values[number, f : f + 1, :] = found[f] + part[number, f : f + 1, :]


def place_kernel(incoming, near, rim, lines, pick, taken, updated, *parts):
    blocks = incoming.shape[0]
    width_y = near.shape[2]
    each = blocks // len(parts)
    placed = None
    for first_block, part in zip(range(0, blocks, each), parts):
        for number in range(first_block, first_block + each):
            span = slice(number * LANES, (number + 1) * LANES)
            column = (number - first_block) * LANES
            value = incoming[number]
            upper = value.astype(jnp.bfloat16).astype(jnp.float32)
            lower = value - upper
            for f in range(FIELDS):
                for values, start in ((upper, column), (lower, column + each * LANES)):
                    wide = jnp.broadcast_to(values[f : f + 1], (16, LANES)).astype(jnp.bfloat16)
                    for first in range(0, INNER, 16):
                        part[f * INNER + first : f * INNER + first + 16, start : start + LANES] = (
                            lines[first : first + 16, span] * wide
                        )
        chosen = pick[first_block * LANES : (first_block + each) * LANES]
        found = jnp.dot(
            part[...], jnp.concatenate([chosen, chosen], axis=0), preferred_element_type=jnp.float32
        )
        placed = found if placed is None else placed + found
    for plane in range(4):
        rows = (plane % 2) * width_y
        lanes = slice((plane // 2) * LANES, (plane // 2 + 1) * LANES)
        free = taken[rows : rows + width_y, lanes] < 0.5
        for f in range(FIELDS):
            value = placed[f * INNER + rows : f * INNER + rows + width_y, lanes]
            if plane in (0, 3):
                at_row = 0 if plane == 0 else width_y
                updated[plane, f] = jnp.where(free, rim[f, at_row : at_row + width_y], value)
                continue
            updated[plane, f] = jnp.where(free, near[plane - 1, f], value)
            for at_row, y_line in ((63 + plane, 0), (65 + plane, width_y - 1)):
                one = slice(y_line, y_line + 1)
                updated[plane, f, one] = jnp.where(
                    free[one], rim[f, at_row : at_row + 1], value[one]
                )


def swap(axis, even, odd):
    count = lax.axis_size(axis)
    out = []
    for first, lines in ((0, even), (1, odd)):
        pairs = [(i, i + 1) for i in range(first, count - 1, 2)]
        out.append(lax.ppermute(lines, axis, pairs + [(j, i) for i, j in pairs]))
    return out


def shards(
    flow_state,
    source,
    diag_scale,
    flux_jac,
    line_coupling,
    block_inverse,
    active_order,
    active_units,
    donor_cells,
    donor_weights,
    receptor_cells,
):
    f32, i32 = jnp.float32, jnp.int32
    vmem = pl.BlockSpec(memory_space=pltpu.VMEM)
    like = jax.ShapeDtypeStruct
    params = pltpu.CompilerParams(vmem_limit_bytes=32 << 20)
    flow = jnp.transpose(flow_state, (0, 2, 1, 3))
    source = jnp.transpose(source, (0, 2, 1, 3))
    jac = jnp.transpose(flux_jac, (1, 0, 2))
    coupling = jnp.transpose(line_coupling, (1, 0, 2))
    width_x, fields, width_y, length = flow.shape
    cells = donor_cells.reshape(donor_cells.shape[2:])
    weights = donor_weights.reshape(donor_weights.shape[2:])
    receptor = receptor_cells.reshape(receptor_cells.shape[2:])
    blocks = receptor.shape[0]

    outside = pl.BlockSpec(memory_space=pltpu.HBM)
    raw = [
        array if array is active_units else pltpu.with_memory_space_constraint(array, pltpu.HBM)
        for array in (
            jac, coupling, block_inverse, active_units, active_order.reshape(1, LANES),
            receptor, flow, source, diag_scale, cells, weights,
        )
    ]
    *edges, flow, source, diag, cells, weights, live, lines, pick, taken, matrices = pl.pallas_call(
        load_kernel,
        out_shape=[like((fields, width_y, length), f32)] * 2
        + [like((fields, width_x, length), f32)] * 2
        + [like(array.shape, array.dtype) for array in raw[6:]]
        + [
            like((LANES, LANES), f32),
            like((INNER, blocks * LANES), jnp.bfloat16),
            like((blocks * LANES, 2 * LANES), jnp.bfloat16),
            like((INNER, 2 * LANES), f32),
            like((8 * fields * fields, length), f32),
        ],
        in_specs=[outside] * 11,
        out_specs=[vmem] * 14,
        scratch_shapes=[
            pltpu.SMEM(jac.shape, f32),
            pltpu.SMEM(coupling.shape, f32),
            pltpu.SMEM(block_inverse.shape, f32),
            pltpu.SMEM(active_units.shape, i32),
            pltpu.VMEM((1, LANES), i32),
            pltpu.VMEM(receptor.shape, i32),
            pltpu.SemaphoreType.DMA((11,)),
        ],
        compiler_params=params,
        name="load_block",
    )(*raw)
    halos = swap("blk", *edges[:2]) + swap("bal", *edges[2:])
    part, near, *rest = pl.pallas_call(
        inner_kernel,
        out_shape=[
            like((blocks, fields, length), f32),
            like((2, fields, width_y, length), f32),
            like((fields, RIM, length), f32),
            like((RIM, length), f32),
            like((RIM, length), f32),
            like((fields, RIM, length), f32),
            like(cells.shape, i32),
            like(cells.shape, f32),
        ],
        in_specs=[vmem] * 7,
        out_specs=[vmem] * 8,
        scratch_shapes=[
            pltpu.VMEM(cells.shape, i32),
            pltpu.VMEM(cells.shape, f32),
            pltpu.VMEM((fields * HALF, 4 * LANES), jnp.bfloat16),
            pltpu.VMEM((4, INNER, LANES), i32),
            pltpu.VMEM((fields, 8, LANES), f32),
        ],
        cost_estimate=pl.CostEstimate(
            flops=10**10, bytes_accessed=3 * 10**6, transcendentals=0
        ),
        compiler_params=params,
        name="inner_lines",
    )(
        matrices, flow, source, diag, live, cells, weights,
    )
    values, rim = pl.pallas_call(
        rim_kernel,
        out_shape=[
            like((blocks, fields, length), f32),
            like((fields, RIM, length), f32),
        ],
        in_specs=[vmem] * 12,
        out_specs=[vmem] * 2,
        scratch_shapes=[
            pltpu.VMEM((fields, RIM, length), f32),
            pltpu.VMEM((fields * (RIM - HALF), 4 * LANES), jnp.bfloat16),
            pltpu.VMEM((4, RIM, LANES), i32),
            pltpu.VMEM((fields, 8, LANES), f32),
        ],
        compiler_params=params,
        name="rim_lines",
    )(matrices, *halos, part, *rest)
    incoming = lax.all_to_all(values, "blk", split_axis=0, concat_axis=0, tiled=True)
    updated = pl.pallas_call(
        place_kernel,
        out_shape=like(flow.shape, f32),
        in_specs=[vmem] * 6,
        out_specs=vmem,
        scratch_shapes=[pltpu.VMEM((fields * INNER, 2 * blocks * LANES // PARTS), jnp.bfloat16)] * PARTS,
        compiler_params=params,
        name="place_receptors",
    )(incoming, near, rim, lines, pick, taken)
    return jnp.transpose(updated, (0, 2, 1, 3))


def solution(mesh):
    placed = (
        P("blk", "bal", None, None),
        P("blk", "bal", None, None),
        P("blk", "bal", None),
        P(),
        P(),
        P(),
        P("blk", "bal", None),
        P("blk", "bal"),
        P("blk", "bal", None, None, None),
        P("blk", "bal", None, None, None),
        P("blk", "bal", None, None),
    )
    return jax.shard_map(
        shards, mesh=mesh, in_specs=placed, out_specs=P("blk", "bal", None, None), check_vma=False
    )
```

```python
import functools

import jax
import jax.numpy as jnp
from jax import lax
from jax.experimental import pallas as pl
from jax.experimental.pallas import tpu as pltpu
from jax.sharding import PartitionSpec as P

SWEEPS = 4
FIELDS = 6
DONORS = 8
LANES = 128
INNER = 64
RIM = 72
HALF = 32
BY_MATRIX = 4
STEPS = 1048000.0
PARTS = 8


def entry(number, f, g):
    row = (number * FIELDS + f) * FIELDS + g
    return slice(row, row + 1)


def apply(matrix, values):
    out = []
    for f in range(FIELDS):
        total = matrix(f, 0) * values[0]
        for g in range(1, FIELDS):
            total = total + matrix(f, g) * values[g]
        out.append(total)
    return out


def solve(residual, scale_inv, matrices):
    lane = lax.broadcasted_iota(jnp.int32, residual[0].shape, 1)
    first, last = lane == 0, lane == LANES - 1
    base = apply(lambda f, g: matrices[entry(3, f, g)], residual)
    base = [value * scale_inv for value in base]
    correction = base
    for _ in range(SWEEPS - 1):
        total = [None] * FIELDS
        for g in range(FIELDS):
            down = jnp.where(first, 0.0, pltpu.roll(correction[g], 1, 1))
            up = jnp.where(last, 0.0, pltpu.roll(correction[g], LANES - 1, 1))
            for f in range(FIELDS):
                term = matrices[entry(1, f, g)] * down + matrices[entry(2, f, g)] * up
                total[f] = term if g == 0 else total[f] + term
        correction = [base[f] - scale_inv * total[f] for f in range(FIELDS)]
    return correction


def fill_table(table, first, half, values):
    high = values.astype(jnp.bfloat16)
    low = (values - high.astype(jnp.float32)).astype(jnp.bfloat16)
    rows = slice(first, first + values.shape[0])
    table[rows, half * LANES : (half + 1) * LANES] = high
    table[rows, (half + 2) * LANES : (half + 3) * LANES] = low


def fill_words(words, scales, corrected):
    whole = []
    for f in range(FIELDS):
        largest = jnp.max(jnp.max(jnp.abs(corrected(f)), axis=0, keepdims=True), axis=1, keepdims=True)
        scale = jnp.broadcast_to(jnp.maximum(largest, 1e-30), (8, LANES))
        scales[f] = scale * (1.0 / (STEPS * 2048.0))
        factor = (STEPS / scale)[0:1]
        whole.append(jnp.round(corrected(f) * factor).astype(jnp.int32))
    parts = []
    for f in (4, 5):
        upper = (whole[f] + 512) >> 10
        parts += [upper, whole[f] - (upper << 10)]
    for word in range(4):
        words[word] = (whole[word] << 11) + parts[word]


def gather_by_lane(words, rows, cell, share, total):
    below = lax.broadcasted_iota(jnp.int32, (8, LANES), 0)
    cell = jnp.broadcast_to(cell, (8, LANES))
    pos = cell & (LANES - 1)
    line = (cell >> 7) - below
    share = jnp.where((line & 7) == 0, jnp.broadcast_to(share, (8, LANES)), 0.0)
    hit = [None] * 4
    for first in range(0, rows, 8):
        chosen = line == first
        for word in range(4):
            found = jnp.take_along_axis(
                words[word, first : first + 8], pos, axis=1, mode="promise_in_bounds"
            )
            hit[word] = found if first == 0 else jnp.where(chosen, found, hit[word])
    low = [(value << 21).astype(jnp.float32) for value in hit]
    found = [value.astype(jnp.float32) for value in hit]
    found += [low[0] + low[1] * (1.0 / 1024), low[2] + low[3] * (1.0 / 1024)]
    return [
        value * share if total is None else total[f] + value * share
        for f, value in enumerate(found)
    ]


def small(numbers):
    return numbers.astype(jnp.float32).astype(jnp.bfloat16)


def gather(table, words, scales, rows, cells, shares, number):
    at_cell = small(lax.broadcasted_iota(jnp.int32, (2 * LANES, 2 * LANES), 0))
    at_line = lax.broadcasted_iota(jnp.int32, (rows - HALF, 2 * LANES), 0)
    one, zero = jnp.bfloat16(1), jnp.bfloat16(0)
    extra = rows - 2 * HALF
    total = [None] * FIELDS
    for k in range(0, BY_MATRIX, 2):
        cell = jnp.concatenate([cells[k + i, pl.ds(number, 1), :] for i in (0, 1)], axis=1)
        share = jnp.concatenate([shares[k + i, pl.ds(number, 1), :] for i in (0, 1)], axis=1)
        column = ((cell >> 5) & LANES) + (cell & (LANES - 1))
        line = ((cell >> 7) & (HALF - 1)) + ((cell >> 8) & HALF)
        pick = jnp.where(at_cell == small(column), one, zero)
        found = jnp.dot(
            table[...], jnp.concatenate([pick, pick], axis=0), preferred_element_type=jnp.float32
        )
        weight = jnp.where(at_line == line, share, 0.0)
        for f in range(FIELDS):
            part = found[f * HALF : (f + 1) * HALF] * weight[:HALF]
            part = jnp.sum(part.reshape(HALF // 8, 8, 2 * LANES), axis=0)
            if extra:
                first = FIELDS * HALF + f * extra
                part = part + found[first : first + extra] * weight[HALF:]
            total[f] = part if k == 0 else total[f] + part
    by_lane = None
    for k in range(BY_MATRIX, DONORS):
        by_lane = gather_by_lane(
            words, rows, cells[k, pl.ds(number, 1), :], shares[k, pl.ds(number, 1), :], by_lane
        )
    return [
        jnp.sum(
            value[:, :LANES] + value[:, LANES:] + by_lane[f] * scales[f], axis=0, keepdims=True
        )
        for f, value in enumerate(total)
    ]


def prepare(receptor, lines, pick, taken):
    at_line = lax.broadcasted_iota(jnp.int32, (INNER, LANES), 0)
    at_cell = lax.broadcasted_iota(jnp.int32, (LANES, LANES), 1)
    for number in range(receptor.shape[0]):
        cell = receptor[number : number + 1, :]
        line = cell >> 7
        where = ((line >> 6) << 7) + (cell & (LANES - 1))
        span = slice(number * LANES, (number + 1) * LANES)
        lines[:, span] = jnp.where(at_line == (line & (INNER - 1)), 1.0, 0.0).astype(jnp.bfloat16)
        where = jnp.transpose(jnp.broadcast_to(where, (LANES, LANES)))
        for half in (0, 1):
            pick[span, half * LANES : (half + 1) * LANES] = jnp.where(
                at_cell + half * LANES == where, 1.0, 0.0
            ).astype(jnp.bfloat16)
    taken[...] = jnp.dot(lines[...], pick[...], preferred_element_type=jnp.float32)


def load_kernel(
    jac_in, coupling_in, inverse_in, units_in, order_in, receptor_in,
    flow_in, source_in, diag_in, cells_in, weights_in,
    x_even, x_odd, y_even, y_odd, flow, source, diag, cells, weights,
    live, lines, pick, taken, matrices,
    jac, coupling, inverse, units, order, receptor, done,
):
    width_x, _, width_y, _ = flow.shape
    copies = [
        pltpu.make_async_copy(origin, target, done.at[number])
        for number, (origin, target) in enumerate(
            (
                (jac_in, jac),
                (coupling_in, coupling),
                (inverse_in, inverse),
                (units_in, units),
                (order_in, order),
                (receptor_in, receptor),
                (flow_in, flow),
                (source_in, source),
                (diag_in, diag),
                (cells_in, cells),
                (weights_in, weights),
            )
        )
    ]
    for copy in copies:
        copy.start()
    for copy in copies[:6]:
        copy.wait()
    for f in range(FIELDS):
        for g in range(FIELDS):
            values = [jac[f, 0, g] + jac[f, 1, g] + jac[f, 2, g] + jac[f, 3, g]]
            for side in (0, 1):
                total = inverse[f, 0] * coupling[0, side, g]
                for h in range(1, FIELDS):
                    total = total + inverse[f, h] * coupling[h, side, g]
                values.append(total)
            values.append(inverse[f, g])
            values += [jac[f, side, g] for side in range(4)]
            for number, value in enumerate(values):
                matrices[entry(number, f, g)] = jnp.full((1, LANES), value, jnp.float32)
    line = lax.broadcasted_iota(jnp.int32, (LANES, LANES), 0)
    place = lax.broadcasted_iota(jnp.int32, (LANES, LANES), 1)
    hit = (line == order[...]) & (place < units[0, 0] * 32)
    live[...] = jnp.broadcast_to(
        jnp.max(jnp.where(hit, 1.0, 0.0), axis=1, keepdims=True), (LANES, LANES)
    )
    prepare(receptor, lines, pick, taken)
    copies[6].wait()
    upward = lax.rem(lax.axis_index("blk"), 2) == 0
    x_even[...] = jnp.where(upward, flow[width_x - 1], flow[0])
    x_odd[...] = jnp.where(upward, flow[0], flow[width_x - 1])
    upward = lax.rem(lax.axis_index("bal"), 2) == 0
    for f in range(FIELDS):
        for x in range(width_x):
            head, tail = flow[x, f, 0:1], flow[x, f, width_y - 1 : width_y]
            y_even[f, x : x + 1] = jnp.where(upward, tail, head)
            y_odd[f, x : x + 1] = jnp.where(upward, head, tail)
    for copy in copies[7:]:
        copy.wait()


def inner_kernel(
    matrices, flow, source, diag, live, cells, weights,
    values, near, rim_residual, rim_scale, rim_live, rim_flow, rim_cells, rim_shares,
    inner_cells, inner_shares, table, words, scales,
):
    width_y = flow.shape[2]
    blocks = cells.shape[1]
    row = lax.broadcasted_iota(jnp.int32, (width_y, LANES), 0)

    cell = cells[...]
    at = cell >> 7
    x, y = at >> 5, at & 31
    middle = (x == 1) | (x == 2)
    edge = middle & ((y == 0) | (y == width_y - 1))
    pos = cell & (LANES - 1)
    inner = middle & ~edge
    inner_cells[...] = (((at - 32) & (INNER - 1)) << 7) + pos
    on_edge = 64 + (x - 1) + jnp.where(y == 0, 0, 2)
    on_rim = jnp.where(x == 0, at, (at - 64) & 63)
    rim_cells[...] = (jnp.where(edge, on_edge, on_rim) << 7) + pos
    weight = weights[...]
    share = weight / jnp.sum(weight, axis=0, keepdims=True)
    inner_shares[...] = jnp.where(inner, share, 0.0)
    rim_shares[...] = jnp.where(inner, 0.0, share)

    def residual_of(plane):
        total = [source[plane, f] for f in range(FIELDS)]
        for g in range(FIELDS):
            here = flow[plane, g]
            left = flow[plane - 1, g] if plane > 0 else None
            right = flow[plane + 1, g] if plane < 3 else None
            before = jnp.where(row == 0, 0.0, pltpu.roll(here, 1, 0))
            after = jnp.where(row == width_y - 1, 0.0, pltpu.roll(here, width_y - 1, 0))
            for f in range(FIELDS):
                value = total[f] - matrices[entry(0, f, g)] * here
                if left is not None:
                    value = value + matrices[entry(4, f, g)] * left
                if right is not None:
                    value = value + matrices[entry(5, f, g)] * right
                total[f] = value + matrices[entry(6, f, g)] * before + matrices[entry(7, f, g)] * after
        return total

    for number, plane in enumerate((0, 3)):
        residual = residual_of(plane)
        rows = slice(number * width_y, (number + 1) * width_y)
        for f in range(FIELDS):
            rim_residual[f, rows] = residual[f]
            rim_flow[f, rows] = flow[plane, f]
        rim_scale[rows] = 1.0 / diag[plane]
        rim_live[rows] = live[plane * width_y : (plane + 1) * width_y]
    rim_scale[RIM - 8 : RIM] = jnp.ones((8, LANES), jnp.float32)
    rim_live[RIM - 8 : RIM] = jnp.zeros((8, LANES), jnp.float32)
    for f in range(FIELDS):
        rim_residual[f, RIM - 8 : RIM] = jnp.zeros((8, LANES), jnp.float32)
        rim_flow[f, RIM - 8 : RIM] = jnp.zeros((8, LANES), jnp.float32)
    for number, plane in enumerate((1, 2)):
        residual = residual_of(plane)
        scale = 1.0 / diag[plane]
        alive = live[plane * width_y : (plane + 1) * width_y]
        for at_row, y_line in ((64 + number, 0), (66 + number, width_y - 1)):
            for f in range(FIELDS):
                rim_residual[f, at_row : at_row + 1] = residual[f][y_line : y_line + 1]
                rim_flow[f, at_row : at_row + 1] = flow[plane, f, y_line : y_line + 1]
            rim_scale[at_row : at_row + 1] = scale[y_line : y_line + 1]
            rim_live[at_row : at_row + 1] = alive[y_line : y_line + 1]
        correction = solve(residual, scale, matrices)
        for f in range(FIELDS):
            corrected = flow[plane, f] + jnp.where(alive > 0.5, correction[f], 0.0)
            near[number, f] = corrected
            fill_table(table, f * HALF, number, corrected)

    fill_words(
        words, scales, lambda f: jnp.concatenate([near[0, f], near[1, f]], axis=0)
    )

    @pl.loop(0, blocks, unroll=16)
    def _(number):
        found = gather(table, words, scales, INNER, inner_cells, inner_shares, number)
        for f in range(FIELDS):
            values[number, f : f + 1, :] = found[f]


def rim_kernel(
    matrices, x_even, x_odd, y_odd, y_even,
    part, rim_residual, rim_scale, rim_live, rim_flow, rim_cells, shares,
    values, rim, residual, table, words, scales,
):
    width_y = x_even.shape[1]
    x_upward = lax.rem(lax.axis_index("blk"), 2) == 0
    y_upward = lax.rem(lax.axis_index("bal"), 2) == 0
    blocks = rim_cells.shape[1]
    for number, (side, halo) in enumerate(((0, (x_odd, x_even)), (1, (x_even, x_odd)))):
        rows = slice(number * width_y, (number + 1) * width_y)
        lines = [jnp.where(x_upward, halo[0][g], halo[1][g]) for g in range(FIELDS)]
        added = apply(lambda f, g: matrices[entry(4 + side, f, g)], lines)
        for f in range(FIELDS):
            residual[f, rows] = rim_residual[f, rows] + added[f]
    for number, (side, halo) in enumerate(((2, (y_odd, y_even)), (3, (y_even, y_odd)))):
        lines = [jnp.where(y_upward, halo[0][g], halo[1][g]) for g in range(FIELDS)]
        added = apply(lambda f, g: matrices[entry(4 + side, f, g)], lines)
        for f in range(FIELDS):
            at_row = 64 + 2 * number
            residual[f, at_row : at_row + 2] = (
                rim_residual[f, at_row : at_row + 2] + added[f][1:3]
            )
            for at_row, x in ((number * (width_y - 1), 0), (width_y + number * (width_y - 1), 3)):
                residual[f, at_row : at_row + 1] = (
                    residual[f, at_row : at_row + 1] + added[f][x : x + 1]
                )
    for f in range(FIELDS):
        residual[f, RIM - 4 : RIM] = jnp.zeros((4, LANES), jnp.float32)
    edges = []
    for half, rows in enumerate((slice(0, 32), slice(32, 64), slice(64, RIM))):
        correction = solve(
            [residual[f, rows] for f in range(FIELDS)], rim_scale[rows], matrices
        )
        alive = rim_live[rows] > 0.5
        for f in range(FIELDS):
            corrected = rim_flow[f, rows] + jnp.where(alive, correction[f], 0.0)
            rim[f, rows] = corrected
            if half < 2:
                fill_table(table, f * HALF, half, corrected)
            else:
                edges.append(corrected)
    edges = jnp.concatenate(edges, axis=0)
    fill_table(table, FIELDS * HALF, 0, edges)
    fill_table(table, FIELDS * HALF, 1, jnp.zeros_like(edges))
    fill_words(words, scales, lambda f: rim[f])

    @pl.loop(0, blocks, unroll=16)
    def _(number):
        found = gather(table, words, scales, RIM, rim_cells, shares, number)
        for f in range(FIELDS):
            values[number, f : f + 1, :] = found[f] + part[number, f : f + 1, :]


def place_kernel(incoming, near, rim, lines, pick, taken, updated, *parts):
    blocks = incoming.shape[0]
    width_y = near.shape[2]
    each = blocks // len(parts)
    placed = None
    for first_block, part in zip(range(0, blocks, each), parts):
        for number in range(first_block, first_block + each):
            span = slice(number * LANES, (number + 1) * LANES)
            column = (number - first_block) * LANES
            value = incoming[number]
            upper = value.astype(jnp.bfloat16).astype(jnp.float32)
            lower = value - upper
            for f in range(FIELDS):
                for values, start in ((upper, column), (lower, column + each * LANES)):
                    wide = jnp.broadcast_to(values[f : f + 1], (16, LANES)).astype(jnp.bfloat16)
                    for first in range(0, INNER, 16):
                        part[f * INNER + first : f * INNER + first + 16, start : start + LANES] = (
                            lines[first : first + 16, span] * wide
                        )
        chosen = pick[first_block * LANES : (first_block + each) * LANES]
        found = jnp.dot(
            part[...], jnp.concatenate([chosen, chosen], axis=0), preferred_element_type=jnp.float32
        )
        placed = found if placed is None else placed + found
    for plane in range(4):
        rows = (plane % 2) * width_y
        lanes = slice((plane // 2) * LANES, (plane // 2 + 1) * LANES)
        free = taken[rows : rows + width_y, lanes] < 0.5
        for f in range(FIELDS):
            value = placed[f * INNER + rows : f * INNER + rows + width_y, lanes]
            if plane in (0, 3):
                at_row = 0 if plane == 0 else width_y
                updated[plane, f] = jnp.where(free, rim[f, at_row : at_row + width_y], value)
                continue
            updated[plane, f] = jnp.where(free, near[plane - 1, f], value)
            for at_row, y_line in ((63 + plane, 0), (65 + plane, width_y - 1)):
                one = slice(y_line, y_line + 1)
                updated[plane, f, one] = jnp.where(
                    free[one], rim[f, at_row : at_row + 1], value[one]
                )


def swap(axis, even, odd):
    count = lax.axis_size(axis)
    out = []
    for first, lines in ((0, even), (1, odd)):
        pairs = [(i, i + 1) for i in range(first, count - 1, 2)]
        out.append(lax.ppermute(lines, axis, pairs + [(j, i) for i, j in pairs]))
    return out


def shards(
    flow_state,
    source,
    diag_scale,
    flux_jac,
    line_coupling,
    block_inverse,
    active_order,
    active_units,
    donor_cells,
    donor_weights,
    receptor_cells,
):
    f32, i32 = jnp.float32, jnp.int32
    vmem = pl.BlockSpec(memory_space=pltpu.VMEM)
    like = jax.ShapeDtypeStruct
    params = pltpu.CompilerParams(vmem_limit_bytes=32 << 20)
    flow = jnp.transpose(flow_state, (0, 2, 1, 3))
    source = jnp.transpose(source, (0, 2, 1, 3))
    jac = jnp.transpose(flux_jac, (1, 0, 2))
    coupling = jnp.transpose(line_coupling, (1, 0, 2))
    width_x, fields, width_y, length = flow.shape
    cells = donor_cells.reshape(donor_cells.shape[2:])
    weights = donor_weights.reshape(donor_weights.shape[2:])
    receptor = receptor_cells.reshape(receptor_cells.shape[2:])
    blocks = receptor.shape[0]

    outside = pl.BlockSpec(memory_space=pltpu.HBM)
    raw = [
        array if array is active_units else pltpu.with_memory_space_constraint(array, pltpu.HBM)
        for array in (
            jac, coupling, block_inverse, active_units, active_order.reshape(1, LANES),
            receptor, flow, source, diag_scale, cells, weights,
        )
    ]
    *edges, flow, source, diag, cells, weights, live, lines, pick, taken, matrices = pl.pallas_call(
        load_kernel,
        out_shape=[like((fields, width_y, length), f32)] * 2
        + [like((fields, width_x, length), f32)] * 2
        + [like(array.shape, array.dtype) for array in raw[6:]]
        + [
            like((LANES, LANES), f32),
            like((INNER, blocks * LANES), jnp.bfloat16),
            like((blocks * LANES, 2 * LANES), jnp.bfloat16),
            like((INNER, 2 * LANES), f32),
            like((8 * fields * fields, length), f32),
        ],
        in_specs=[outside] * 11,
        out_specs=[vmem] * 14,
        scratch_shapes=[
            pltpu.SMEM(jac.shape, f32),
            pltpu.SMEM(coupling.shape, f32),
            pltpu.SMEM(block_inverse.shape, f32),
            pltpu.SMEM(active_units.shape, i32),
            pltpu.VMEM((1, LANES), i32),
            pltpu.VMEM(receptor.shape, i32),
            pltpu.SemaphoreType.DMA((11,)),
        ],
        compiler_params=params,
        name="load_block",
    )(*raw)
    halos = swap("blk", *edges[:2]) + swap("bal", *edges[2:])[::-1]
    part, near, *rest = pl.pallas_call(
        inner_kernel,
        out_shape=[
            like((blocks, fields, length), f32),
            like((2, fields, width_y, length), f32),
            like((fields, RIM, length), f32),
            like((RIM, length), f32),
            like((RIM, length), f32),
            like((fields, RIM, length), f32),
            like(cells.shape, i32),
            like(cells.shape, f32),
        ],
        in_specs=[vmem] * 7,
        out_specs=[vmem] * 8,
        scratch_shapes=[
            pltpu.VMEM(cells.shape, i32),
            pltpu.VMEM(cells.shape, f32),
            pltpu.VMEM((fields * HALF, 4 * LANES), jnp.bfloat16),
            pltpu.VMEM((4, INNER, LANES), i32),
            pltpu.VMEM((fields, 8, LANES), f32),
        ],
        cost_estimate=pl.CostEstimate(
            flops=10**10, bytes_accessed=3 * 10**6, transcendentals=0
        ),
        compiler_params=params,
        name="inner_lines",
    )(
        matrices, flow, source, diag, live, cells, weights,
    )
    values, rim = pl.pallas_call(
        rim_kernel,
        out_shape=[
            like((blocks, fields, length), f32),
            like((fields, RIM, length), f32),
        ],
        in_specs=[vmem] * 12,
        out_specs=[vmem] * 2,
        scratch_shapes=[
            pltpu.VMEM((fields, RIM, length), f32),
            pltpu.VMEM((fields * (RIM - HALF), 4 * LANES), jnp.bfloat16),
            pltpu.VMEM((4, RIM, LANES), i32),
            pltpu.VMEM((fields, 8, LANES), f32),
        ],
        compiler_params=params,
        name="rim_lines",
    )(matrices, *halos, part, *rest)
    incoming = lax.all_to_all(values, "blk", split_axis=0, concat_axis=0, tiled=True)
    updated = pl.pallas_call(
        place_kernel,
        out_shape=like(flow.shape, f32),
        in_specs=[vmem] * 6,
        out_specs=vmem,
        scratch_shapes=[pltpu.VMEM((fields * INNER, 2 * blocks * LANES // PARTS), jnp.bfloat16)] * PARTS,
        compiler_params=params,
        name="place_receptors",
    )(incoming, near, rim, lines, pick, taken)
    return jnp.transpose(updated, (0, 2, 1, 3))


def solution(mesh):
    placed = (
        P("blk", "bal", None, None),
        P("blk", "bal", None, None),
        P("blk", "bal", None),
        P(),
        P(),
        P(),
        P("blk", "bal", None),
        P("blk", "bal"),
        P("blk", "bal", None, None, None),
        P("blk", "bal", None, None, None),
        P("blk", "bal", None, None),
    )
    return jax.shard_map(
        shards, mesh=mesh, in_specs=placed, out_specs=P("blk", "bal", None, None), check_vma=False
    )
```

```python
import functools

import jax
import jax.numpy as jnp
from jax import lax
from jax.experimental import pallas as pl
from jax.experimental.pallas import tpu as pltpu
from jax.sharding import PartitionSpec as P

SWEEPS = 4
FIELDS = 6
DONORS = 8
LANES = 128
INNER = 64
RIM = 72
HALF = 32
BY_MATRIX = 4
STEPS = 1048000.0
PARTS = 8


def entry(number, f, g):
    row = (number * FIELDS + f) * FIELDS + g
    return slice(row, row + 1)


def apply(matrix, values):
    out = []
    for f in range(FIELDS):
        total = matrix(f, 0) * values[0]
        for g in range(1, FIELDS):
            total = total + matrix(f, g) * values[g]
        out.append(total)
    return out


def solve(residual, scale_inv, matrices):
    lane = lax.broadcasted_iota(jnp.int32, residual[0].shape, 1)
    first, last = lane == 0, lane == LANES - 1
    base = apply(lambda f, g: matrices[entry(3, f, g)], residual)
    base = [value * scale_inv for value in base]
    correction = base
    for _ in range(SWEEPS - 1):
        total = [None] * FIELDS
        for g in range(FIELDS):
            down = jnp.where(first, 0.0, pltpu.roll(correction[g], 1, 1))
            up = jnp.where(last, 0.0, pltpu.roll(correction[g], LANES - 1, 1))
            for f in range(FIELDS):
                term = matrices[entry(1, f, g)] * down + matrices[entry(2, f, g)] * up
                total[f] = term if g == 0 else total[f] + term
        correction = [base[f] - scale_inv * total[f] for f in range(FIELDS)]
    return correction


def fill_table(table, first, half, values):
    high = values.astype(jnp.bfloat16)
    low = (values - high.astype(jnp.float32)).astype(jnp.bfloat16)
    rows = slice(first, first + values.shape[0])
    table[rows, half * LANES : (half + 1) * LANES] = high
    table[rows, (half + 2) * LANES : (half + 3) * LANES] = low


def fill_words(words, scales, corrected):
    whole = []
    for f in range(FIELDS):
        largest = jnp.max(jnp.max(jnp.abs(corrected(f)), axis=0, keepdims=True), axis=1, keepdims=True)
        scale = jnp.broadcast_to(jnp.maximum(largest, 1e-30), (8, LANES))
        scales[f] = scale * (1.0 / (STEPS * 2048.0))
        factor = (STEPS / scale)[0:1]
        whole.append(jnp.round(corrected(f) * factor).astype(jnp.int32))
    parts = []
    for f in (4, 5):
        upper = (whole[f] + 512) >> 10
        parts += [upper, whole[f] - (upper << 10)]
    for word in range(4):
        words[word] = (whole[word] << 11) + parts[word]


def gather_by_lane(words, rows, cell, share, total):
    below = lax.broadcasted_iota(jnp.int32, (8, LANES), 0)
    cell = jnp.broadcast_to(cell, (8, LANES))
    pos = cell & (LANES - 1)
    line = (cell >> 7) - below
    share = jnp.where((line & 7) == 0, jnp.broadcast_to(share, (8, LANES)), 0.0)
    hit = [None] * 4
    for first in range(0, rows, 8):
        chosen = line == first
        for word in range(4):
            found = jnp.take_along_axis(
                words[word, first : first + 8], pos, axis=1, mode="promise_in_bounds"
            )
            hit[word] = found if first == 0 else jnp.where(chosen, found, hit[word])
    low = [(value << 21).astype(jnp.float32) for value in hit]
    found = [value.astype(jnp.float32) for value in hit]
    found += [low[0] + low[1] * (1.0 / 1024), low[2] + low[3] * (1.0 / 1024)]
    return [
        value * share if total is None else total[f] + value * share
        for f, value in enumerate(found)
    ]


def small(numbers):
    return numbers.astype(jnp.float32).astype(jnp.bfloat16)


def gather(table, words, scales, rows, cells, shares, number):
    at_cell = small(lax.broadcasted_iota(jnp.int32, (2 * LANES, 2 * LANES), 0))
    at_line = lax.broadcasted_iota(jnp.int32, (rows - HALF, 2 * LANES), 0)
    one, zero = jnp.bfloat16(1), jnp.bfloat16(0)
    extra = rows - 2 * HALF
    total = [None] * FIELDS
    for k in range(0, BY_MATRIX, 2):
        cell = jnp.concatenate([cells[k + i, pl.ds(number, 1), :] for i in (0, 1)], axis=1)
        share = jnp.concatenate([shares[k + i, pl.ds(number, 1), :] for i in (0, 1)], axis=1)
        column = ((cell >> 5) & LANES) + (cell & (LANES - 1))
        line = ((cell >> 7) & (HALF - 1)) + ((cell >> 8) & HALF)
        pick = jnp.where(at_cell == small(column), one, zero)
        found = jnp.dot(
            table[...], jnp.concatenate([pick, pick], axis=0), preferred_element_type=jnp.float32
        )
        weight = jnp.where(at_line == line, share, 0.0)
        for f in range(FIELDS):
            part = found[f * HALF : (f + 1) * HALF] * weight[:HALF]
            part = jnp.sum(part.reshape(HALF // 8, 8, 2 * LANES), axis=0)
            if extra:
                first = FIELDS * HALF + f * extra
                part = part + found[first : first + extra] * weight[HALF:]
            total[f] = part if k == 0 else total[f] + part
    by_lane = None
    for k in range(BY_MATRIX, DONORS):
        by_lane = gather_by_lane(
            words, rows, cells[k, pl.ds(number, 1), :], shares[k, pl.ds(number, 1), :], by_lane
        )
    return [
        jnp.sum(
            value[:, :LANES] + value[:, LANES:] + by_lane[f] * scales[f], axis=0, keepdims=True
        )
        for f, value in enumerate(total)
    ]


def prepare(receptor, lines, pick, taken):
    at_line = lax.broadcasted_iota(jnp.int32, (INNER, LANES), 0)
    at_cell = lax.broadcasted_iota(jnp.int32, (LANES, LANES), 1)
    for number in range(receptor.shape[0]):
        cell = receptor[number : number + 1, :]
        line = cell >> 7
        where = ((line >> 6) << 7) + (cell & (LANES - 1))
        span = slice(number * LANES, (number + 1) * LANES)
        lines[:, span] = jnp.where(at_line == (line & (INNER - 1)), 1.0, 0.0).astype(jnp.bfloat16)
        where = jnp.transpose(jnp.broadcast_to(where, (LANES, LANES)))
        for half in (0, 1):
            pick[span, half * LANES : (half + 1) * LANES] = jnp.where(
                at_cell + half * LANES == where, 1.0, 0.0
            ).astype(jnp.bfloat16)
    taken[...] = jnp.dot(lines[...], pick[...], preferred_element_type=jnp.float32)


def load_kernel(
    jac_in, coupling_in, inverse_in, units_in, order_in, receptor_in,
    flow_in, source_in, diag_in, cells_in, weights_in,
    x_even, x_odd, y_even, y_odd, flow, source, diag, cells, weights,
    live, lines, pick, taken, matrices,
    jac, coupling, inverse, units, order, receptor, done,
):
    width_x, _, width_y, _ = flow.shape
    copies = [
        pltpu.make_async_copy(origin, target, done.at[number])
        for number, (origin, target) in enumerate(
            (
                (jac_in, jac),
                (coupling_in, coupling),
                (inverse_in, inverse),
                (units_in, units),
                (order_in, order),
                (receptor_in, receptor),
                (flow_in, flow),
                (source_in, source),
                (diag_in, diag),
                (cells_in, cells),
                (weights_in, weights),
            )
        )
    ]
    for copy in copies:
        copy.start()
    for copy in copies[:6]:
        copy.wait()
    for f in range(FIELDS):
        for g in range(FIELDS):
            values = [jac[f, 0, g] + jac[f, 1, g] + jac[f, 2, g] + jac[f, 3, g]]
            for side in (0, 1):
                total = inverse[f, 0] * coupling[0, side, g]
                for h in range(1, FIELDS):
                    total = total + inverse[f, h] * coupling[h, side, g]
                values.append(total)
            values.append(inverse[f, g])
            values += [jac[f, side, g] for side in range(4)]
            for number, value in enumerate(values):
                matrices[entry(number, f, g)] = jnp.full((1, LANES), value, jnp.float32)
    line = lax.broadcasted_iota(jnp.int32, (LANES, LANES), 0)
    place = lax.broadcasted_iota(jnp.int32, (LANES, LANES), 1)
    hit = (line == order[...]) & (place < units[0, 0] * 32)
    live[...] = jnp.broadcast_to(
        jnp.max(jnp.where(hit, 1.0, 0.0), axis=1, keepdims=True), (LANES, LANES)
    )
    prepare(receptor, lines, pick, taken)
    copies[6].wait()
    upward = lax.rem(lax.axis_index("blk"), 2) == 0
    x_even[...] = jnp.where(upward, flow[width_x - 1], flow[0])
    x_odd[...] = jnp.where(upward, flow[0], flow[width_x - 1])
    upward = lax.rem(lax.axis_index("bal"), 2) == 0
    for f in range(FIELDS):
        for x in range(width_x):
            head, tail = flow[x, f, 0:1], flow[x, f, width_y - 1 : width_y]
            y_even[f, x : x + 1] = jnp.where(upward, tail, head)
            y_odd[f, x : x + 1] = jnp.where(upward, head, tail)
    for copy in copies[7:]:
        copy.wait()


def inner_kernel(
    matrices, flow, source, diag, live, cells, weights,
    values, near, rim_residual, rim_scale, rim_live, rim_flow, rim_cells, rim_shares,
    inner_cells, inner_shares, table, words, scales,
):
    width_y = flow.shape[2]
    blocks = cells.shape[1]
    row = lax.broadcasted_iota(jnp.int32, (width_y, LANES), 0)

    cell = cells[...]
    at = cell >> 7
    x, y = at >> 5, at & 31
    middle = (x == 1) | (x == 2)
    edge = middle & ((y == 0) | (y == width_y - 1))
    pos = cell & (LANES - 1)
    inner = middle & ~edge
    inner_cells[...] = (((at - 32) & (INNER - 1)) << 7) + pos
    on_edge = 64 + (x - 1) + jnp.where(y == 0, 0, 2)
    on_rim = jnp.where(x == 0, at, (at - 64) & 63)
    rim_cells[...] = (jnp.where(edge, on_edge, on_rim) << 7) + pos
    weight = weights[...]
    share = weight / jnp.sum(weight, axis=0, keepdims=True)
    inner_shares[...] = jnp.where(inner, share, 0.0)
    rim_shares[...] = jnp.where(inner, 0.0, share)

    def residual_of(plane):
        total = [source[plane, f] for f in range(FIELDS)]
        for g in range(FIELDS):
            here = flow[plane, g]
            left = flow[plane - 1, g] if plane > 0 else None
            right = flow[plane + 1, g] if plane < 3 else None
            before = jnp.where(row == 0, 0.0, pltpu.roll(here, 1, 0))
            after = jnp.where(row == width_y - 1, 0.0, pltpu.roll(here, width_y - 1, 0))
            for f in range(FIELDS):
                value = total[f] - matrices[entry(0, f, g)] * here
                if left is not None:
                    value = value + matrices[entry(4, f, g)] * left
                if right is not None:
                    value = value + matrices[entry(5, f, g)] * right
                total[f] = value + matrices[entry(6, f, g)] * before + matrices[entry(7, f, g)] * after
        return total

    for number, plane in enumerate((0, 3)):
        residual = residual_of(plane)
        rows = slice(number * width_y, (number + 1) * width_y)
        for f in range(FIELDS):
            rim_residual[f, rows] = residual[f]
            rim_flow[f, rows] = flow[plane, f]
        rim_scale[rows] = 1.0 / diag[plane]
        rim_live[rows] = live[plane * width_y : (plane + 1) * width_y]
    rim_scale[RIM - 8 : RIM] = jnp.ones((8, LANES), jnp.float32)
    rim_live[RIM - 8 : RIM] = jnp.zeros((8, LANES), jnp.float32)
    for f in range(FIELDS):
        rim_residual[f, RIM - 8 : RIM] = jnp.zeros((8, LANES), jnp.float32)
        rim_flow[f, RIM - 8 : RIM] = jnp.zeros((8, LANES), jnp.float32)
    for number, plane in enumerate((1, 2)):
        residual = residual_of(plane)
        scale = 1.0 / diag[plane]
        alive = live[plane * width_y : (plane + 1) * width_y]
        for at_row, y_line in ((64 + number, 0), (66 + number, width_y - 1)):
            for f in range(FIELDS):
                rim_residual[f, at_row : at_row + 1] = residual[f][y_line : y_line + 1]
                rim_flow[f, at_row : at_row + 1] = flow[plane, f, y_line : y_line + 1]
            rim_scale[at_row : at_row + 1] = scale[y_line : y_line + 1]
            rim_live[at_row : at_row + 1] = alive[y_line : y_line + 1]
        correction = solve(residual, scale, matrices)
        for f in range(FIELDS):
            corrected = flow[plane, f] + jnp.where(alive > 0.5, correction[f], 0.0)
            near[number, f] = corrected
            fill_table(table, f * HALF, number, corrected)

    fill_words(
        words, scales, lambda f: jnp.concatenate([near[0, f], near[1, f]], axis=0)
    )

    @pl.loop(0, blocks, unroll=16)
    def _(number):
        found = gather(table, words, scales, INNER, inner_cells, inner_shares, number)
        for f in range(FIELDS):
            values[number, f : f + 1, :] = found[f]


def rim_kernel(
    matrices, x_odd, x_even, y_odd, y_even,
    part, rim_residual, rim_scale, rim_live, rim_flow, rim_cells, shares,
    values, rim, residual, table, words, scales,
):
    width_y = x_even.shape[1]
    x_upward = lax.rem(lax.axis_index("blk"), 2) == 0
    y_upward = lax.rem(lax.axis_index("bal"), 2) == 0
    blocks = rim_cells.shape[1]
    for number, (side, halo) in enumerate(((0, (x_odd, x_even)), (1, (x_even, x_odd)))):
        rows = slice(number * width_y, (number + 1) * width_y)
        lines = [jnp.where(x_upward, halo[0][g], halo[1][g]) for g in range(FIELDS)]
        added = apply(lambda f, g: matrices[entry(4 + side, f, g)], lines)
        for f in range(FIELDS):
            residual[f, rows] = rim_residual[f, rows] + added[f]
    for number, (side, halo) in enumerate(((2, (y_odd, y_even)), (3, (y_even, y_odd)))):
        lines = [jnp.where(y_upward, halo[0][g], halo[1][g]) for g in range(FIELDS)]
        added = apply(lambda f, g: matrices[entry(4 + side, f, g)], lines)
        for f in range(FIELDS):
            at_row = 64 + 2 * number
            residual[f, at_row : at_row + 2] = (
                rim_residual[f, at_row : at_row + 2] + added[f][1:3]
            )
            for at_row, x in ((number * (width_y - 1), 0), (width_y + number * (width_y - 1), 3)):
                residual[f, at_row : at_row + 1] = (
                    residual[f, at_row : at_row + 1] + added[f][x : x + 1]
                )
    for f in range(FIELDS):
        residual[f, RIM - 4 : RIM] = jnp.zeros((4, LANES), jnp.float32)
    edges = []
    for half, rows in enumerate((slice(0, 32), slice(32, 64), slice(64, RIM))):
        correction = solve(
            [residual[f, rows] for f in range(FIELDS)], rim_scale[rows], matrices
        )
        alive = rim_live[rows] > 0.5
        for f in range(FIELDS):
            corrected = rim_flow[f, rows] + jnp.where(alive, correction[f], 0.0)
            rim[f, rows] = corrected
            if half < 2:
                fill_table(table, f * HALF, half, corrected)
            else:
                edges.append(corrected)
    edges = jnp.concatenate(edges, axis=0)
    fill_table(table, FIELDS * HALF, 0, edges)
    fill_table(table, FIELDS * HALF, 1, jnp.zeros_like(edges))
    fill_words(words, scales, lambda f: rim[f])

    @pl.loop(0, blocks, unroll=16)
    def _(number):
        found = gather(table, words, scales, RIM, rim_cells, shares, number)
        for f in range(FIELDS):
            values[number, f : f + 1, :] = found[f] + part[number, f : f + 1, :]


def place_kernel(incoming, near, rim, lines, pick, taken, updated, *parts):
    blocks = incoming.shape[0]
    width_y = near.shape[2]
    each = blocks // len(parts)
    placed = None
    for first_block, part in zip(range(0, blocks, each), parts):
        for number in range(first_block, first_block + each):
            span = slice(number * LANES, (number + 1) * LANES)
            column = (number - first_block) * LANES
            value = incoming[number]
            upper = value.astype(jnp.bfloat16).astype(jnp.float32)
            lower = value - upper
            for f in range(FIELDS):
                for values, start in ((upper, column), (lower, column + each * LANES)):
                    wide = jnp.broadcast_to(values[f : f + 1], (16, LANES)).astype(jnp.bfloat16)
                    for first in range(0, INNER, 16):
                        part[f * INNER + first : f * INNER + first + 16, start : start + LANES] = (
                            lines[first : first + 16, span] * wide
                        )
        chosen = pick[first_block * LANES : (first_block + each) * LANES]
        found = jnp.dot(
            part[...], jnp.concatenate([chosen, chosen], axis=0), preferred_element_type=jnp.float32
        )
        placed = found if placed is None else placed + found
    for plane in range(4):
        rows = (plane % 2) * width_y
        lanes = slice((plane // 2) * LANES, (plane // 2 + 1) * LANES)
        free = taken[rows : rows + width_y, lanes] < 0.5
        for f in range(FIELDS):
            value = placed[f * INNER + rows : f * INNER + rows + width_y, lanes]
            if plane in (0, 3):
                at_row = 0 if plane == 0 else width_y
                updated[plane, f] = jnp.where(free, rim[f, at_row : at_row + width_y], value)
                continue
            updated[plane, f] = jnp.where(free, near[plane - 1, f], value)
            for at_row, y_line in ((63 + plane, 0), (65 + plane, width_y - 1)):
                one = slice(y_line, y_line + 1)
                updated[plane, f, one] = jnp.where(
                    free[one], rim[f, at_row : at_row + 1], value[one]
                )


def swap(axis, even, odd):
    count = lax.axis_size(axis)
    out = []
    for first, lines in ((0, even), (1, odd)):
        pairs = [(i, i + 1) for i in range(first, count - 1, 2)]
        out.append(lax.ppermute(lines, axis, pairs + [(j, i) for i, j in pairs]))
    return out


def shards(
    flow_state,
    source,
    diag_scale,
    flux_jac,
    line_coupling,
    block_inverse,
    active_order,
    active_units,
    donor_cells,
    donor_weights,
    receptor_cells,
):
    f32, i32 = jnp.float32, jnp.int32
    vmem = pl.BlockSpec(memory_space=pltpu.VMEM)
    like = jax.ShapeDtypeStruct
    params = pltpu.CompilerParams(vmem_limit_bytes=32 << 20)
    flow = jnp.transpose(flow_state, (0, 2, 1, 3))
    source = jnp.transpose(source, (0, 2, 1, 3))
    jac = jnp.transpose(flux_jac, (1, 0, 2))
    coupling = jnp.transpose(line_coupling, (1, 0, 2))
    width_x, fields, width_y, length = flow.shape
    cells = donor_cells.reshape(donor_cells.shape[2:])
    weights = donor_weights.reshape(donor_weights.shape[2:])
    receptor = receptor_cells.reshape(receptor_cells.shape[2:])
    blocks = receptor.shape[0]

    outside = pl.BlockSpec(memory_space=pltpu.HBM)
    raw = [
        array if array is active_units else pltpu.with_memory_space_constraint(array, pltpu.HBM)
        for array in (
            jac, coupling, block_inverse, active_units, active_order.reshape(1, LANES),
            receptor, flow, source, diag_scale, cells, weights,
        )
    ]
    *edges, flow, source, diag, cells, weights, live, lines, pick, taken, matrices = pl.pallas_call(
        load_kernel,
        out_shape=[like((fields, width_y, length), f32)] * 2
        + [like((fields, width_x, length), f32)] * 2
        + [like(array.shape, array.dtype) for array in raw[6:]]
        + [
            like((LANES, LANES), f32),
            like((INNER, blocks * LANES), jnp.bfloat16),
            like((blocks * LANES, 2 * LANES), jnp.bfloat16),
            like((INNER, 2 * LANES), f32),
            like((8 * fields * fields, length), f32),
        ],
        in_specs=[outside] * 11,
        out_specs=[vmem] * 14,
        scratch_shapes=[
            pltpu.SMEM(jac.shape, f32),
            pltpu.SMEM(coupling.shape, f32),
            pltpu.SMEM(block_inverse.shape, f32),
            pltpu.SMEM(active_units.shape, i32),
            pltpu.VMEM((1, LANES), i32),
            pltpu.VMEM(receptor.shape, i32),
            pltpu.SemaphoreType.DMA((11,)),
        ],
        compiler_params=params,
        name="load_block",
    )(*raw)
    halos = swap("blk", *edges[:2])[::-1] + swap("bal", *edges[2:])[::-1]
    part, near, *rest = pl.pallas_call(
        inner_kernel,
        out_shape=[
            like((blocks, fields, length), f32),
            like((2, fields, width_y, length), f32),
            like((fields, RIM, length), f32),
            like((RIM, length), f32),
            like((RIM, length), f32),
            like((fields, RIM, length), f32),
            like(cells.shape, i32),
            like(cells.shape, f32),
        ],
        in_specs=[vmem] * 7,
        out_specs=[vmem] * 8,
        scratch_shapes=[
            pltpu.VMEM(cells.shape, i32),
            pltpu.VMEM(cells.shape, f32),
            pltpu.VMEM((fields * HALF, 4 * LANES), jnp.bfloat16),
            pltpu.VMEM((4, INNER, LANES), i32),
            pltpu.VMEM((fields, 8, LANES), f32),
        ],
        cost_estimate=pl.CostEstimate(
            flops=10**10, bytes_accessed=3 * 10**6, transcendentals=0
        ),
        compiler_params=params,
        name="inner_lines",
    )(
        matrices, flow, source, diag, live, cells, weights,
    )
    values, rim = pl.pallas_call(
        rim_kernel,
        out_shape=[
            like((blocks, fields, length), f32),
            like((fields, RIM, length), f32),
        ],
        in_specs=[vmem] * 12,
        out_specs=[vmem] * 2,
        scratch_shapes=[
            pltpu.VMEM((fields, RIM, length), f32),
            pltpu.VMEM((fields * (RIM - HALF), 4 * LANES), jnp.bfloat16),
            pltpu.VMEM((4, RIM, LANES), i32),
            pltpu.VMEM((fields, 8, LANES), f32),
        ],
        compiler_params=params,
        name="rim_lines",
    )(matrices, *halos, part, *rest)
    incoming = lax.all_to_all(values, "blk", split_axis=0, concat_axis=0, tiled=True)
    updated = pl.pallas_call(
        place_kernel,
        out_shape=like(flow.shape, f32),
        in_specs=[vmem] * 6,
        out_specs=vmem,
        scratch_shapes=[pltpu.VMEM((fields * INNER, 2 * blocks * LANES // PARTS), jnp.bfloat16)] * PARTS,
        compiler_params=params,
        name="place_receptors",
    )(incoming, near, rim, lines, pick, taken)
    return jnp.transpose(updated, (0, 2, 1, 3))


def solution(mesh):
    placed = (
        P("blk", "bal", None, None),
        P("blk", "bal", None, None),
        P("blk", "bal", None),
        P(),
        P(),
        P(),
        P("blk", "bal", None),
        P("blk", "bal"),
        P("blk", "bal", None, None, None),
        P("blk", "bal", None, None, None),
        P("blk", "bal", None, None),
    )
    return jax.shard_map(
        shards, mesh=mesh, in_specs=placed, out_specs=P("blk", "bal", None, None), check_vma=False
    )
```
